256 devices in a mesh: samp: 16 (over z, x_lo), tok: 16 (over x_hi, y, core).
Axes of the slice: x: 4 (x_hi: 2, x_lo: 2; x = x_hi * 2 + x_lo), y: 4, z: 8, core: 2. Of those that a mesh axis runs over, the one named last changes fastest.
Arguments:
- features_in: bfloat16 [16, 256, 512, 128], P('samp', 'tok'), may hold values from -6 to 6
- path_noise: bfloat16 [16, 256, 512, 128], P('samp', 'tok'), may hold values from -6 to 6
- latent: float32 [16, 512], P('samp'), may hold values from -6 to 6
- bank: bfloat16 [8, 9, 128, 128], replicated, may hold values from -0.1875 to 0.1875
- style_weight: float32 [512, 128], replicated, may hold values from -0.25 to 0.25
- select_weight: float32 [512, 8], replicated, may hold values from -0.25 to 0.25
- path_mean: float32 [1], replicated, may hold values from 0.5 to 2
Outputs:
- features: bfloat16 [16, 256, 512, 128], P('samp', 'tok')
- penalty: float32 [16], P('samp')
- bank_grad: float32 [8, 9, 128, 128], P(None, None, 'samp')
- style_grad: float32 [512, 128], replicated
- select_grad: float32 [512, 8], replicated
The draws below stay inside these ranges and needn't reach their ends.
All inputs are finite; a program needn't handle non-finite values.
Results may differ from the reference program's by a relative error of at most 0.0049.
Values may be sent and summed in bfloat16 or wider, within the bound.
No kernel may reach another device: no remote copies, remote signals or barrier semaphores. Data moves between devices by JAX's collectives and lax.ppermute only.
A program may use at most 128 MiB of HBM per device.

```python
import math
import jax
import jax.numpy as jnp
from jax import lax

C = 128
NB = 8
WD = 512
TAPS = 9
WPX = 512
H = 256
IMAGES = 16


def level_of(rng, extent, shards, smallest, largest):
    level, own = 1.0, jax.random.fold_in(rng, 6)
    for position, shards_of in shards:
        heights = jnp.exp(jax.random.uniform(jax.random.fold_in(own, position), (shards_of,), jnp.float32, smallest / len(shards), largest / len(shards)))
        level = level * jnp.repeat(heights, extent[position] // shards_of).reshape([-1 if axis == position else 1 for axis in range(len(extent))])
    return level


def bell_draw(key, extent, width, limit, cuts=(), kind=jnp.bfloat16):
    entries = jax.random.normal(key, extent, jnp.float32) * width
    if len(cuts) > 0:
        entries = level_of(key, extent, cuts, -0.22, 0.18) * entries
    return jnp.clip(entries, min=-limit, max=limit).astype(kind)


def setup_inputs(seed: int = 0) -> dict:
    keys = jax.random.split(jax.random.key(seed), 8)
    return {
        "features_in": bell_draw(keys[0], (IMAGES, H, WPX, C), 1.0, 6.0, ((0, 16), (1, 16))),
        "path_noise": bell_draw(keys[1], (IMAGES, H, WPX, C), 1.0, 6.0, ((0, 16), (1, 16))),
        "latent": bell_draw(keys[2], (IMAGES, WD), 1.0, 6.0, ((0, 16),), jnp.float32),
        "bank": bell_draw(keys[3], (NB, TAPS, C, C), (TAPS * C) ** -0.5, 0.1875),
        "style_weight": bell_draw(keys[4], (WD, C), WD ** -0.5, 0.25, (), jnp.float32),
        "select_weight": bell_draw(keys[5], (WD, NB), WD ** -0.5, 0.25, (), jnp.float32),
        "path_mean": jnp.clip(jax.random.uniform(keys[6], (1,), jnp.float32, 0.5, 2.0), 0.5, 2.0),
    }


HIGH = lax.Precision.HIGHEST

def mixing(wvec, select_w):
    logits = jnp.dot(wvec, select_w, precision=HIGH)
    expo = jnp.exp(logits)
    return expo / jnp.sum(expo)

def modulate(wvec, kern, style_w):
    style = jnp.dot(wvec, style_w, precision=HIGH) + 1.0
    scaled = kern * style[None, :, None]
    demod = lax.rsqrt(lax.optimization_barrier(jnp.sum(scaled * scaled, axis=(0, 1))) + 1e-08)
    return scaled * demod[None, None, :]

def kernel_of(wvec, bank32, style_w, select_w):
    mixed = jnp.einsum('b,bkio->kio', mixing(wvec, select_w), bank32, precision=HIGH)
    return modulate(wvec, mixed, style_w)

def path_grad(wvec, corr_one, bank32, style_w, select_w):
    return jax.grad(lambda v: jnp.sum(corr_one * kernel_of(v, bank32, style_w, select_w)))(wvec)

def penalty_of(wvec, corr_one, bank32, style_w, select_w, target):
    grad_w = path_grad(wvec, corr_one, bank32, style_w, select_w)
    length = jnp.sqrt(jnp.sum(grad_w * grad_w) + 1e-08)
    return (length - target) ** 2

def reference(features_in, path_noise, latent, bank, style_weight, select_weight, path_mean):
    bank32 = bank.astype(jnp.float32)
    kernels = jax.vmap(kernel_of, (0, None, None, None))(latent, bank32, style_weight, select_weight)
    kernel_low = kernels.astype(jnp.bfloat16)
    scale = 1.0 / math.sqrt(H * WPX)

    def one_image(items):
        image, noise, kern = items
        padded = jnp.pad(image, ((1, 1), (1, 1), (0, 0)))
        flat_noise = noise.reshape(-1, C)
        total = jnp.zeros((H * WPX, C), jnp.float32)
        corr_taps = []
        for tap in range(TAPS):
            ky, kx = (tap // 3, tap % 3)
            window = padded[ky:ky + H, kx:kx + WPX, :].reshape(-1, C)
            total = total + jnp.dot(window, kern[tap], preferred_element_type=jnp.float32)
            corr_taps.append(jnp.dot(window.T, flat_noise, preferred_element_type=jnp.float32))
        return (total.reshape(H, WPX, C).astype(jnp.bfloat16), jnp.stack(corr_taps, 0) * scale)
    features, corr = lax.map(one_image, (features_in, path_noise, kernel_low))
    target = path_mean[0]

    def pens_fn(bank_f, style_w, select_w):
        return jax.vmap(penalty_of, (0, 0, None, None, None, None))(latent, corr, bank_f, style_w, select_w, target)
    pens, back = jax.vjp(pens_fn, bank32, style_weight, select_weight)
    weights = jnp.full((IMAGES,), 1.0 / IMAGES, jnp.float32)
    bank_grad, style_grad, select_grad = back(weights)
    return (features, pens, bank_grad, style_grad, select_grad)
```

```python
import math

import jax
import jax.numpy as jnp
from jax import lax
from jax.sharding import PartitionSpec as P

HIGH = lax.Precision.HIGHEST
EPS = 1e-08


def dot(a, b):
    return jnp.dot(a, b, precision=HIGH)


def soften(logits):
    expo = jnp.exp(logits)
    return expo / jnp.sum(expo)


def mix(weights, bank32):
    return jnp.einsum("b,bkio->kio", weights, bank32, precision=HIGH)


def kernel_parts(vec, bank32, style_w, select_w):
    share = soften(dot(vec, select_w))
    style = dot(vec, style_w) + 1.0
    mixed = mix(share, bank32)
    scaled = mixed * style[None, :, None]
    demod = lax.rsqrt(jnp.sum(scaled * scaled, axis=(0, 1)) + EPS)
    return share, style, mixed, scaled, demod


def halo_rows(block):
    count = lax.axis_size("tok")
    forward = [(i, i + 1) for i in range(count - 1)]
    backward = [(i + 1, i) for i in range(count - 1)]
    rows = block.shape[1]
    low = lax.ppermute(block[:, rows - 1 :], "tok", forward)
    high = lax.ppermute(block[:, :1], "tok", backward)
    return low, high


def conv_and_corr(features_in, path_noise, kernel_low):
    count, rows, cols, chans = features_in.shape
    low, high = halo_rows(features_in)
    padded = jnp.concatenate([low, features_in, high], axis=1)
    padded = jnp.pad(padded, ((0, 0), (0, 0), (1, 1), (0, 0)))
    total = jnp.zeros((count, rows, cols, chans), jnp.float32)
    taps = []
    for tap in range(9):
        ky, kx = (tap // 3, tap % 3)
        window = padded[:, ky : ky + rows, kx : kx + cols, :]
        total = total + jnp.einsum(
            "nrci,io->nrco", window, kernel_low[tap], preferred_element_type=jnp.float32
        )
        taps.append(
            jnp.einsum("nrci,nrco->io", window, path_noise, preferred_element_type=jnp.float32)
        )
    return total.astype(jnp.bfloat16), jnp.stack(taps)


def sum_over_tok(part):
    count = lax.axis_size("tok")
    chips = count // 2
    core = lax.axis_index("tok") % 2
    swap = [(i, i ^ 1) for i in range(count)]
    groups = [[2 * i + c for i in range(chips)] for c in range(2)]
    flat = part.reshape(2, -1, 128)
    keep = lax.dynamic_index_in_dim(flat, core, 0, keepdims=False)
    give = lax.dynamic_index_in_dim(flat, 1 - core, 0, keepdims=False)
    half = keep + lax.ppermute(give, "tok", swap)
    size = half.shape[0] // chips
    pieces = lax.all_to_all(
        half.reshape(chips, size, 128), "tok", 0, 0, axis_index_groups=groups
    )
    piece = jnp.sum(pieces, axis=0)
    spread = jnp.broadcast_to(piece[None], (chips, size, 128))
    mine = lax.all_to_all(spread, "tok", 0, 0, axis_index_groups=groups).reshape(-1, 128)
    other = lax.ppermute(mine, "tok", swap)
    first = jnp.where(core == 0, mine, other)
    second = jnp.where(core == 0, other, mine)
    return jnp.concatenate([first, second]).reshape(part.shape)


def split_two(x):
    high = x.astype(jnp.bfloat16)
    low = (x - high.astype(jnp.float32)).astype(jnp.bfloat16)
    return high, low


def local(features_in, path_noise, latent, bank, style_weight, select_weight, path_mean):
    count, rows, cols, chans = features_in.shape
    images = lax.axis_size("samp")
    height = rows * lax.axis_size("tok")
    vec = latent[0]
    bank32 = bank.astype(jnp.float32)
    share, style, mixed, scaled, demod = kernel_parts(vec, bank32, style_weight, select_weight)
    kernel_low = (scaled * demod).astype(jnp.bfloat16)
    features, part = conv_and_corr(features_in, path_noise, kernel_low)
    corr = sum_over_tok(part) * (1.0 / math.sqrt(height * cols))

    demod3 = demod * demod * demod
    along = jnp.sum(corr * scaled, axis=(0, 1))
    proj = demod * corr - (demod3 * along) * scaled
    by_style = jnp.sum(proj * mixed, axis=(0, 2))
    proj_s = proj * style[None, :, None]
    by_share = jnp.einsum("kio,bkio->b", proj_s, bank32, precision=HIGH)
    by_logit = share * (by_share - jnp.sum(share * by_share))
    grad_v = dot(style_weight, by_style) + dot(select_weight, by_logit)
    length = jnp.sqrt(jnp.sum(grad_v * grad_v) + EPS)
    gap = length - path_mean[0]
    factor = (2.0 / images) * gap / length

    d_style = dot(grad_v, style_weight)
    d_logit = dot(grad_v, select_weight)
    mean_d = jnp.sum(share * d_logit)
    d_share = share * (d_logit - mean_d)
    d_mixed = mix(d_share, bank32)
    d_scaled = d_mixed * style[None, :, None] + mixed * d_style[None, :, None]
    cross = jnp.sum(scaled * d_scaled, axis=(0, 1))
    turn = jnp.sum(corr * d_scaled, axis=(0, 1))
    row_p = -demod * demod * cross
    row_d = -demod3 * along
    row_k = 2.0 * demod3 * demod * demod * along * cross - demod3 * turn
    second = row_p * proj + row_d * d_scaled + row_k * scaled
    to_style = jnp.sum(second * mixed + proj * d_mixed, axis=(0, 2))
    to_mixed = second * style[None, :, None] + proj * d_style[None, :, None]
    to_share = jnp.einsum("kio,bkio->b", to_mixed, bank32, precision=HIGH)
    to_share = to_share + by_share * (d_logit - mean_d) - d_logit * jnp.sum(share * by_share)
    to_logit = share * (to_share - jnp.sum(share * to_share))

    n_taps = corr.shape[0]
    shards = images
    width = chans // shards
    small = jnp.concatenate(
        [
            vec,
            factor * grad_v,
            factor * to_style,
            by_style,
            style,
            d_style,
            row_p,
            row_d,
            row_k,
            jnp.concatenate(
                [factor * to_logit, by_logit, factor * share, factor * d_share, share, d_share]
            ),
            jnp.zeros((80,), jnp.float32),
        ]
    ).reshape(-1, 128)
    small_high, small_low = split_two(small)
    proj_low = proj.astype(jnp.bfloat16).reshape(n_taps, shards, width, chans)
    proj_low = jnp.transpose(proj_low, (1, 0, 2, 3)).reshape(shards, -1, chans)
    smalls = jnp.concatenate([small_high, small_low])
    sent = jnp.concatenate(
        [proj_low, jnp.broadcast_to(smalls[None], (shards,) + smalls.shape)], axis=1
    )
    got = lax.all_to_all(sent, "samp", 0, 0)

    body = n_taps * width
    rest = small.shape[0]
    proj_n = got[:, :body].astype(jnp.float32).reshape(images, n_taps, width, chans)
    small_n = got[:, body : body + rest].astype(jnp.float32) + got[:, body + rest :].astype(
        jnp.float32
    )
    vec_n = small_n[:, 0:4].reshape(images, -1)
    grad_n = small_n[:, 4:8].reshape(images, -1)
    to_style_n, by_style_n = small_n[:, 8], small_n[:, 9]
    shard = lax.axis_index("samp")
    style_n = lax.dynamic_slice_in_dim(small_n[:, 10], shard * width, width, 1)[:, None, :, None]
    d_style_n = lax.dynamic_slice_in_dim(small_n[:, 11], shard * width, width, 1)[:, None, :, None]
    row_p_n, row_d_n, row_k_n = (small_n[:, j][:, None, None, :] for j in (12, 13, 14))
    last = small_n[:, 15]
    to_logit_n, by_logit_n, fshare_n, fd_share_n, share_n, d_share_n = (
        last[:, 8 * j : 8 * j + 8] for j in range(6)
    )
    bank_s = lax.dynamic_slice_in_dim(bank32, shard * width, width, 2)
    both = jnp.concatenate([share_n, d_share_n])
    mixes = jnp.einsum("nb,bkio->nkio", both, bank_s, precision=HIGH)
    mixed_n, d_mixed_n = mixes[:images], mixes[images:]
    scaled_n = mixed_n * style_n
    d_scaled_n = d_mixed_n * style_n + mixed_n * d_style_n
    second_n = row_p_n * proj_n + row_d_n * d_scaled_n + row_k_n * scaled_n
    to_mixed_n = second_n * style_n + proj_n * d_style_n
    to_d_mixed_n = proj_n * style_n
    bank_grad = jnp.einsum(
        "nb,nkio->bkio",
        jnp.concatenate([fshare_n, fd_share_n]),
        jnp.concatenate([to_mixed_n, to_d_mixed_n]),
        precision=HIGH,
    )
    left = jnp.concatenate([vec_n, grad_n]).T
    style_grad = dot(left, jnp.concatenate([to_style_n, by_style_n]))
    select_grad = dot(left, jnp.concatenate([to_logit_n, by_logit_n]))
    penalty = (gap * gap).reshape(1)
    return (features, penalty, bank_grad, style_grad, select_grad)


def solution(mesh):
    placed = (
        P("samp", "tok", None, None),
        P("samp", "tok", None, None),
        P("samp", None),
        P(),
        P(),
        P(),
        P(),
    )
    return jax.shard_map(
        local,
        mesh=mesh,
        in_specs=placed,
        out_specs=(P("samp", "tok", None, None), P("samp"), P(None, None, "samp", None), P(), P()),
        check_vma=False,
    )
```

```python
import math

import jax
import jax.numpy as jnp
from jax import lax
from jax.experimental import pallas as pl
from jax.experimental.pallas import tpu as pltpu
from jax.sharding import PartitionSpec as P

HIGH = lax.Precision.HIGHEST
EPS = 1e-08
F32 = jnp.float32
BF16 = jnp.bfloat16
TAPS = 9
C = 128
NB = 8
GROUP = 4
MIB = 1024 * 1024


def whole(count):
    return [pl.BlockSpec(memory_space=pltpu.VMEM)] * count


def call(kernel, outs, inputs, scratch=(), limit=24, flops=0, name=None):
    size = sum(math.prod(x.shape) * x.dtype.itemsize for x in inputs)
    shapes = [jax.ShapeDtypeStruct(s, d) for s, d in outs]
    return pl.pallas_call(
        kernel,
        out_shape=shapes,
        in_specs=whole(len(inputs)),
        out_specs=whole(len(outs)),
        scratch_shapes=list(scratch),
        compiler_params=pltpu.CompilerParams(vmem_limit_bytes=limit * MIB),
        cost_estimate=pl.CostEstimate(flops=flops, bytes_accessed=size, transcendentals=0),
        name=name,
    )(*inputs)


def row_dot(row, mat):
    rows = jnp.broadcast_to(row, (8, row.shape[1]))
    return jnp.dot(rows, mat, precision=HIGH, preferred_element_type=F32)[:1]


def row_dot_t(row, mat):
    rows = jnp.broadcast_to(row, (8, row.shape[1]))
    return lax.dot_general(
        rows, mat, (((1,), (1,)), ((), ())), precision=HIGH, preferred_element_type=F32
    )[:1]


def down(row):
    return jnp.broadcast_to(row, (C, C)).T


def across(col):
    size = col.shape[0]
    lane = lax.broadcasted_iota(jnp.int32, (size, C), 1)
    line = lax.broadcasted_iota(jnp.int32, (size, C), 0)
    return jnp.sum(jnp.where(lane == line, col, 0.0), axis=0, keepdims=True)


def widen(row):
    return jnp.concatenate([row, jnp.zeros((1, C - row.shape[1]), F32)], axis=1)


def weighted(bank, weights, tap):
    total = weights[:, 0:1] * bank[0, tap].astype(F32)
    for b in range(1, NB):
        total = total + weights[:, b : b + 1] * bank[b, tap].astype(F32)
    return total


def kernel_maker(latent, bank, style_w, select_w, mixed, scaled, taps, rows):
    vec = latent[...]
    expo = jnp.exp(row_dot(vec, select_w[...]))
    share = expo / jnp.sum(expo, axis=1, keepdims=True)
    style = row_dot(vec, style_w[...]) + 1.0
    style_d = down(style)
    power = jnp.zeros((1, C), F32)
    for tap in range(TAPS):
        one = weighted(bank, share, tap)
        mixed[tap] = one
        one = one * style_d
        scaled[tap] = one
        power = power + jnp.sum(one * one, axis=0, keepdims=True)
    demod = lax.rsqrt(power + EPS)
    zero = jnp.zeros((C, C), BF16)
    for line in range(4):
        for out in range(2):
            for kx in range(3):
                ky = line - out
                at = (3 * out + kx) * C
                if 0 <= ky < 3:
                    block = (scaled[3 * ky + kx] * demod).astype(BF16)
                else:
                    block = zero
                taps[line * C : line * C + C, at : at + C] = block
    rows[0:1] = style
    rows[1:2] = demod
    rows[2:3] = widen(share)
    rows[3:8] = jnp.zeros((5, C), F32)


def corr_kernel(low, block, high, noise, keep, give, acc, flat):
    height, width, _ = block.shape
    group = GROUP
    acc[...] = jnp.zeros_like(acc)
    lane = lax.broadcasted_iota(jnp.int32, (C, group * width), 1) % width

    def step(start, above, here, below):
        side = noise[pl.ds(start, group)].reshape(group * width, C).T
        zero = jnp.zeros_like(side)
        later = jnp.where(lane == width - 1, zero, pltpu.roll(side, group * width - 1, 1))
        former = jnp.where(lane == 0, zero, pltpu.roll(side, 1, 1))
        left = jnp.concatenate([later, side, former], axis=0)
        right = jnp.concatenate([above, here, below], axis=1)
        acc[...] += jnp.dot(left, right, preferred_element_type=F32)

    def lines(start):
        return block[pl.ds(start, group)].reshape(group * width, C)

    rest = (group - 1) * width
    step(
        0,
        jnp.concatenate([low[0], block[0 : group - 1].reshape(rest, C)], axis=0),
        lines(0),
        lines(1),
    )

    @pl.loop(1, height // group - 1, unroll=True)
    def _(index):
        start = index * group
        step(start, lines(start - 1), lines(start), lines(start + 1))

    start = height - group
    step(
        start,
        lines(start - 1),
        lines(start),
        jnp.concatenate([block[start + 1 : height].reshape(rest, C), high[0]], axis=0),
    )
    for ky in range(3):
        for kx in range(3):
            tap = 3 * ky + kx
            flat[tap * C : tap * C + C] = acc[kx * C : kx * C + C, ky * C : ky * C + C].T
    core = lax.axis_index("tok") % 2
    half = TAPS * C // 2
    keep[...] = flat[pl.ds(pl.multiple_of(core * half, 8), half)]
    give[...] = flat[pl.ds(pl.multiple_of((1 - core) * half, 8), half)]


def conv_kernel(low, block, high, taps, out):
    height, width, _ = block.shape
    line = lax.broadcasted_iota(jnp.int32, (width, C), 0)

    def pair(start, lines):
        left = jnp.concatenate(lines, axis=1)
        both = jnp.dot(left, taps[...], preferred_element_type=F32)
        for j in range(2):
            part = both[:, 3 * C * j : 3 * C * j + 3 * C]
            former = jnp.where(line == 0, 0.0, pltpu.roll(part[:, :C], 1, 0))
            later = jnp.where(line == width - 1, 0.0, pltpu.roll(part[:, 2 * C :], width - 1, 0))
            out[start + j] = (former + part[:, C : 2 * C] + later).astype(BF16)

    pair(0, [low[0], block[0], block[1], block[2]])

    @pl.loop(1, height // 2 - 1)
    def _(index):
        start = 2 * index
        pair(start, [block[start - 1], block[start], block[start + 1], block[start + 2]])

    start = height - 2
    pair(start, [block[start - 1], block[start], block[start + 1], high[0]])


def against_bank(bank, terms):
    sums = []
    for b in range(NB):
        total = terms[0] * bank[b, 0].astype(F32)
        for tap in range(1, TAPS):
            total = total + terms[tap] * bank[b, tap].astype(F32)
        sums.append(jnp.sum(total, axis=0, keepdims=True))
    return across(jnp.sum(jnp.concatenate(sums, axis=0), axis=1, keepdims=True))


def image_kernel(
    scale, images, mine, other, mixed, scaled, rows, latent, bank, style_w, select_w, target,
    sent, penalty, corr, proj, terms, d_scaled, d_mixed,
):
    core = lax.axis_index("tok") % 2
    half = TAPS * C // 2
    terms_flat = terms
    terms_flat[pl.ds(pl.multiple_of(core * half, 8), half)] = mine[...] * scale
    terms_flat[pl.ds(pl.multiple_of((1 - core) * half, 8), half)] = other[...] * scale
    for tap in range(TAPS):
        corr[tap] = terms_flat[tap * C : tap * C + C]
    style, demod, share = rows[0:1], rows[1:2], rows[2:3]
    style_d = down(style)
    demod3 = demod * demod * demod
    along = jnp.zeros((1, C), F32)
    for tap in range(TAPS):
        along = along + jnp.sum(corr[tap] * scaled[tap], axis=0, keepdims=True)
    pull = demod3 * along
    total = jnp.zeros((C, C), F32)
    work = terms.reshape(TAPS, C, C)
    for tap in range(TAPS):
        one = demod * corr[tap] - pull * scaled[tap]
        proj[tap] = one
        total = total + one * mixed[tap]
        work[tap] = one * style_d
    by_style = across(jnp.sum(total, axis=1, keepdims=True))
    by_share = against_bank(bank, work)
    inner = jnp.sum(share * by_share, axis=1, keepdims=True)
    by_logit = share * (by_share - inner)
    grad = row_dot_t(by_style, style_w[...]) + row_dot_t(by_logit[:, :NB], select_w[...])
    length = jnp.sqrt(jnp.sum(grad * grad, axis=1, keepdims=True) + EPS)
    gap = length - target[...]
    penalty[...] = gap * gap
    factor = (2.0 / images) * gap / length

    d_style = row_dot(grad, style_w[...])
    d_style_d = down(d_style)
    d_logit = widen(row_dot(grad, select_w[...]))
    mean = jnp.sum(share * d_logit, axis=1, keepdims=True)
    d_share = share * (d_logit - mean)
    cross = jnp.zeros((1, C), F32)
    turn = jnp.zeros((1, C), F32)
    for tap in range(TAPS):
        one = weighted(bank, d_share, tap)
        d_mixed[tap] = one
        one = one * style_d + mixed[tap] * d_style_d
        d_scaled[tap] = one
        cross = cross + jnp.sum(scaled[tap] * one, axis=0, keepdims=True)
        turn = turn + jnp.sum(corr[tap] * one, axis=0, keepdims=True)
    row_p = -demod * demod * cross
    row_d = -pull
    row_k = 2.0 * demod * demod * pull * cross - demod3 * turn
    total = jnp.zeros((C, C), F32)
    for tap in range(TAPS):
        one = row_p * proj[tap] + row_d * d_scaled[tap] + row_k * scaled[tap]
        total = total + one * mixed[tap] + proj[tap] * d_mixed[tap]
        work[tap] = one * style_d + proj[tap] * d_style_d
    to_style = across(jnp.sum(total, axis=1, keepdims=True))
    to_share = against_bank(bank, work) + by_share * (d_logit - mean) - d_logit * inner
    to_logit = share * (to_share - jnp.sum(share * to_share, axis=1, keepdims=True))

    last = jnp.concatenate(
        [
            x[:, :NB]
            for x in (
                factor * to_logit, by_logit, factor * share, factor * d_share, share, d_share,
            )
        ]
        + [jnp.zeros((1, C - 6 * NB), F32)],
        axis=1,
    )
    vec = latent[...]
    small = jnp.concatenate(
        [vec[:, C * j : C * j + C] for j in range(4)]
        + [factor * grad[:, C * j : C * j + C] for j in range(4)]
        + [factor * to_style, by_style, style, d_style, row_p, row_d, row_k, last],
        axis=0,
    )
    high = small.astype(BF16)
    lower = (small - high.astype(F32)).astype(BF16)
    width = C // images
    body = TAPS * width
    pad = sent.shape[1] - body - 32
    for s in range(images):
        pieces = [proj[tap, s * width : s * width + width] for tap in range(TAPS)]
        pieces.append(jnp.zeros((pad, C), F32))
        sent[s, : body + pad] = jnp.concatenate(pieces, axis=0).astype(BF16)
        sent[s, body + pad : body + pad + 16] = high
        sent[s, body + pad + 16 :] = lower


def final_kernel(got, bank_s, bank_grad, style_grad, select_grad, small, flip, to_k, to_dk):
    images = got.shape[0]
    width = C // images
    body = TAPS * width
    first = got.shape[1] - 32
    for n in range(images):
        small[n] = got[n, first : first + 16].astype(F32) + got[n, first + 16 :].astype(F32)
    styles = jnp.concatenate(
        [small[:, 10], small[:, 11], jnp.zeros((C - 2 * images, C), F32)], axis=0
    )
    flip[...] = styles.T
    shard = lax.axis_index("samp")
    style_c = flip[pl.ds(pl.multiple_of(shard * width, 8), width)]
    for n in range(images):
        last = small[n, 15:16]
        style = style_c[:, n : n + 1][None]
        d_style = style_c[:, images + n : images + n + 1][None]
        row_p, row_d, row_k = (small[n, j : j + 1][None] for j in (12, 13, 14))
        proj = got[n, :first].astype(F32)[:body].reshape(TAPS, width, C)
        mixed = last[:, 32:33][None] * bank_s[0]
        d_mixed = last[:, 40:41][None] * bank_s[0]
        for b in range(1, NB):
            mixed = mixed + last[:, 32 + b : 33 + b][None] * bank_s[b]
            d_mixed = d_mixed + last[:, 40 + b : 41 + b][None] * bank_s[b]
        scaled = mixed * style
        d_scaled = d_mixed * style + mixed * d_style
        second = row_p * proj + row_d * d_scaled + row_k * scaled
        to_k[n] = second * style + proj * d_style
        to_dk[n] = proj * style
    for b in range(NB):
        total = jnp.zeros((TAPS, width, C), F32)
        for n in range(images):
            last = small[n, 15:16]
            total = total + last[:, 16 + b : 17 + b][None] * to_k[n]
            total = total + last[:, 24 + b : 25 + b][None] * to_dk[n]
        bank_grad[b] = total
    last = small[:, 15]
    right = jnp.concatenate(
        [
            jnp.concatenate([small[:, 8], last], axis=1),
            jnp.concatenate([small[:, 9], pltpu.roll(last, C - NB, 1)], axis=1),
        ],
        axis=0,
    )
    for j in range(4):
        left = jnp.concatenate([small[:, j], small[:, 4 + j]], axis=0)
        both = lax.dot_general(
            left, right, (((0,), (0,)), ((), ())), precision=HIGH, preferred_element_type=F32
        )
        style_grad[C * j : C * j + C] = both[:, :C]
        select_grad[C * j : C * j + C] = both[:, C : C + NB]


def halo_rows(block):
    count = lax.axis_size("tok")
    forward = [(i, i + 1) for i in range(count - 1)]
    backward = [(i + 1, i) for i in range(count - 1)]
    rows = block.shape[0]
    low = lax.ppermute(block[rows - 1 :], "tok", forward)
    high = lax.ppermute(block[:1], "tok", backward)
    return low, high


def local(features_in, path_noise, latent, bank, style_weight, select_weight, path_mean):
    _, rows, cols, chans = features_in.shape
    images = lax.axis_size("samp")
    toks = lax.axis_size("tok")
    chips = toks // 2
    width = chans // images
    swap = [(i, i ^ 1) for i in range(toks)]
    groups = [[2 * i + c for i in range(chips)] for c in range(2)]
    scale = 1.0 / math.sqrt(rows * toks * cols)
    block, noise = features_in[0], path_noise[0]
    low, high = halo_rows(block)
    cube = (TAPS, C, C)
    mixed, scaled, taps, small = call(
        kernel_maker,
        [(cube, F32), (cube, F32), ((4 * C, 6 * C), BF16), ((8, C), F32)],
        [latent, bank, style_weight, select_weight],
        flops=2_000_000_000,
        name="kernel_maker",
    )
    half = TAPS * C // 2
    keep, give = call(
        corr_kernel,
        [((half, C), F32)] * 2,
        [low, block, high, noise],
        [pltpu.VMEM((3 * C, 3 * C), F32), pltpu.VMEM((TAPS * C, C), F32)],
        flops=4_000_000_000,
        name="corr",
    )
    keep = keep + lax.ppermute(give, "tok", swap)
    size = half // chips
    pieces = lax.all_to_all(
        keep.reshape(chips, size, C), "tok", 0, 0, axis_index_groups=groups
    )
    spread = jnp.broadcast_to(jnp.sum(pieces, axis=0)[None], (chips, size, C))
    mine = lax.all_to_all(spread, "tok", 0, 0, axis_index_groups=groups).reshape(half, C)
    other = lax.ppermute(mine, "tok", swap)
    message = -(-(TAPS * width) // 16) * 16 + 32

    def image(*refs):
        image_kernel(scale, images, *refs)

    sent, penalty = call(
        image,
        [((images, message, C), BF16), ((1, 1), F32)],
        [
            mine, other, mixed, scaled, small, latent, bank, style_weight, select_weight,
            path_mean.reshape(1, 1),
        ],
        [
            pltpu.VMEM(cube, F32),
            pltpu.VMEM(cube, F32),
            pltpu.VMEM((TAPS * C, C), F32),
            pltpu.VMEM(cube, F32),
            pltpu.VMEM(cube, F32),
        ],
        flops=6_000_000_000,
        name="image",
    )
    got = lax.all_to_all(sent, "samp", 0, 0)
    (features,) = call(
        conv_kernel,
        [((rows, cols, C), BF16)],
        [low, block, high, taps],
        flops=5_000_000_000,
        name="conv",
    )
    shard = lax.axis_index("samp")
    bank_s = lax.dynamic_slice_in_dim(bank, shard * width, width, 2).astype(F32)
    bank_grad, style_grad, select_grad = call(
        final_kernel,
        [((NB, TAPS, width, C), F32), (style_weight.shape, F32), (select_weight.shape, F32)],
        [got, bank_s],
        [
            pltpu.VMEM((images, 16, C), F32),
            pltpu.VMEM((C, C), F32),
            pltpu.VMEM((images, TAPS, width, C), F32),
            pltpu.VMEM((images, TAPS, width, C), F32),
        ],
        name="final",
    )
    return (features[None], penalty.reshape(1), bank_grad, style_grad, select_grad)


def solution(mesh):
    placed = (
        P("samp", "tok", None, None),
        P("samp", "tok", None, None),
        P("samp", None),
        P(),
        P(),
        P(),
        P(),
    )
    return jax.shard_map(
        local,
        mesh=mesh,
        in_specs=placed,
        out_specs=(P("samp", "tok", None, None), P("samp"), P(None, None, "samp", None), P(), P()),
        check_vma=False,
    )
```

```python
import math

import jax
import jax.numpy as jnp
from jax import lax
from jax.experimental import pallas as pl
from jax.experimental.pallas import tpu as pltpu
from jax.sharding import PartitionSpec as P

HIGH = lax.Precision.HIGHEST
EPS = 1e-08
F32 = jnp.float32
BF16 = jnp.bfloat16
TAPS = 9
C = 128
NB = 8
GROUP = 4
CORR_LIMIT = 61
MIB = 1024 * 1024


def whole(count):
    return [pl.BlockSpec(memory_space=pltpu.VMEM)] * count


def call(kernel, outs, inputs, scratch=(), limit=10, flops=0, name=None, far=()):
    specs = whole(len(inputs))
    for place in far:
        specs[place] = pl.BlockSpec(memory_space=pltpu.HBM)
    size = sum(math.prod(x.shape) * x.dtype.itemsize for x in inputs)
    shapes = [jax.ShapeDtypeStruct(s, d) for s, d in outs]
    return pl.pallas_call(
        kernel,
        out_shape=shapes,
        in_specs=specs,
        out_specs=whole(len(outs)),
        scratch_shapes=list(scratch),
        compiler_params=pltpu.CompilerParams(vmem_limit_bytes=limit * MIB),
        cost_estimate=pl.CostEstimate(flops=flops, bytes_accessed=size, transcendentals=0),
        name=name,
    )(*inputs)


def row_dot(row, mat):
    rows = jnp.broadcast_to(row, (8, row.shape[1]))
    return jnp.dot(rows, mat, precision=HIGH, preferred_element_type=F32)[:1]


def row_dot_t(row, mat):
    rows = jnp.broadcast_to(row, (8, row.shape[1]))
    return lax.dot_general(
        rows, mat, (((1,), (1,)), ((), ())), precision=HIGH, preferred_element_type=F32
    )[:1]


def down(row):
    return jnp.broadcast_to(row, (C, C)).T


def across(col):
    size = col.shape[0]
    lane = lax.broadcasted_iota(jnp.int32, (size, C), 1)
    line = lax.broadcasted_iota(jnp.int32, (size, C), 0)
    return jnp.sum(jnp.where(lane == line, col, 0.0), axis=0, keepdims=True)


def widen(row):
    return jnp.concatenate([row, jnp.zeros((1, C - row.shape[1]), F32)], axis=1)


def weighted(bank, weights, tap):
    total = weights[:, 0:1] * bank[0, tap].astype(F32)
    for b in range(1, NB):
        total = total + weights[:, b : b + 1] * bank[b, tap].astype(F32)
    return total


def kernel_maker(latent, bank, style_w, select_w, taps, rows, scaled):
    vec = latent[...]
    expo = jnp.exp(row_dot_t(vec, select_w[...]))
    share = expo / jnp.sum(expo, axis=1, keepdims=True)
    style = row_dot(vec, style_w[...]) + 1.0
    style_d = down(style)
    power = jnp.zeros((1, C), F32)
    for tap in range(TAPS):
        one = weighted(bank, share, tap) * style_d
        scaled[tap] = one
        power = power + jnp.sum(one * one, axis=0, keepdims=True)
    demod = lax.rsqrt(power + EPS)
    zero = jnp.zeros((C, C), BF16)
    for line in range(4):
        for out in range(2):
            for kx in range(3):
                ky = line - out
                at = (3 * out + kx) * C
                if 0 <= ky < 3:
                    block = (scaled[3 * ky + kx] * demod).astype(BF16)
                else:
                    block = zero
                taps[line * C : line * C + C, at : at + C] = block
    rows[0:1] = style
    rows[1:2] = demod
    rows[2:3] = widen(share)
    rows[3:8] = jnp.zeros((5, C), F32)


def corr_kernel(block_far, noise_far, flat, edge_low, edge_high, acc, block, noise, sems):
    height, width, _ = block.shape
    group = GROUP
    count = height // group

    def fetch(which, index):
        source, target = ((block_far, block), (noise_far, noise))[which]
        part = pl.ds(index * group, group)
        return pltpu.make_async_copy(source.at[part], target.at[part], sems.at[which, index])

    fetch(0, 0).start()
    for index in range(count):
        if index + 1 < count:
            fetch(0, index + 1).start()
        fetch(1, index).start()
    fetch(0, 0).wait()
    acc[...] = jnp.zeros_like(acc)
    lane = lax.broadcasted_iota(jnp.int32, (C, group * width), 1) % width

    def ready(index):
        if index + 1 < count:
            fetch(0, index + 1).wait()
        fetch(1, index).wait()

    def step(start, above, here, below):
        side = noise[pl.ds(start, group)].reshape(group * width, C).T
        zero = jnp.zeros_like(side)
        later = jnp.where(lane == width - 1, zero, pltpu.roll(side, group * width - 1, 1))
        former = jnp.where(lane == 0, zero, pltpu.roll(side, 1, 1))
        left = jnp.concatenate([later, side, former], axis=0)
        right = jnp.concatenate([above, here, below], axis=1)
        acc[...] += jnp.dot(left, right, preferred_element_type=F32)
        return left

    def lines(start):
        return block[pl.ds(start, group)].reshape(group * width, C)

    rest = (group - 1) * width
    none = jnp.zeros((width, C), BF16)
    ready(0)
    left = step(
        0,
        jnp.concatenate([none, block[0 : group - 1].reshape(rest, C)], axis=0),
        lines(0),
        lines(1),
    )
    edge_low[...] = left[:, :width]

    for index in range(1, count - 1):
        ready(index)
        start = index * group
        step(start, lines(start - 1), lines(start), lines(start + 1))

    start = height - group
    ready(count - 1)
    left = step(
        start,
        lines(start - 1),
        lines(start),
        jnp.concatenate([block[start + 1 : height].reshape(rest, C), none], axis=0),
    )
    edge_high[...] = left[:, rest:]
    for ky in range(3):
        for kx in range(3):
            tap = 3 * ky + kx
            flat[tap * C : tap * C + C] = acc[kx * C : kx * C + C, ky * C : ky * C + C].T


def edge_kernel(near, far, flat, edge_low, edge_high, rows, keep, give, both):
    core = lax.axis_index("tok") % 2
    first = jnp.where(core == 0, far[0], near[0])
    last = jnp.where(core == 0, near[0], far[0])
    above = jnp.dot(edge_low[...], first, preferred_element_type=F32)
    below = jnp.dot(edge_high[...], last, preferred_element_type=F32)
    side = 3 * C
    both[side : 2 * side] = flat[side : 2 * side]
    for kx in range(3):
        at = kx * C
        both[at : at + C] = flat[at : at + C] + above[at : at + C].T
        low = 2 * side + at
        both[low : low + C] = flat[low : low + C] + below[at : at + C].T
    half = TAPS * C // 2
    keep[...] = both[pl.ds(pl.multiple_of(core * half, 8), half)]
    give[...] = both[pl.ds(pl.multiple_of((1 - core) * half, 8), half)]


def conv_kernel(offset, pairs, final, near, far, above, lines, below, taps, *rest):
    out, token = rest[-2:]
    token[...] = jnp.zeros_like(token)
    width = lines.shape[1]
    line = lax.broadcasted_iota(jnp.int32, (width, C), 0)
    core = lax.axis_index("tok") % 2
    place = offset + pl.program_id(0)
    first, last = above[0], below[0]
    if offset == 0:
        first = jnp.where(place == 0, jnp.where(core == 0, far[0], near[0]), first)
    if final:
        last = jnp.where(place == pairs - 1, jnp.where(core == 0, near[0], far[0]), last)
    left = jnp.concatenate([first, lines[0], lines[1], last], axis=1)
    both = jnp.dot(left, taps[...], preferred_element_type=F32)
    for j in range(2):
        part = both[:, 3 * C * j : 3 * C * j + 3 * C]
        former = jnp.where(line == 0, 0.0, pltpu.roll(part[:, :C], 1, 0))
        later = jnp.where(line == width - 1, 0.0, pltpu.roll(part[:, 2 * C :], width - 1, 0))
        out[j] = (former + part[:, C : 2 * C] + later).astype(BF16)


def conv_part(offset, steps, near, far, block, taps, after, done):
    rows, cols, _ = block.shape
    pairs = rows // 2
    one = (1, cols, C)

    def body(*refs):
        conv_kernel(offset, pairs, offset + steps == pairs, *refs)

    specs = [
        pl.BlockSpec(one, lambda g: (0, 0, 0)),
        pl.BlockSpec(one, lambda g: (0, 0, 0)),
        pl.BlockSpec(one, lambda g: (jnp.maximum(2 * (offset + g) - 1, 0), 0, 0)),
        pl.BlockSpec((2, cols, C), lambda g: (offset + g, 0, 0)),
        pl.BlockSpec(one, lambda g: (jnp.minimum(2 * (offset + g) + 2, rows - 1), 0, 0)),
        pl.BlockSpec(taps.shape, lambda g: (0, 0)),
        pl.BlockSpec(memory_space=pl.ANY),
    ]
    inputs = [near, far, block, block, block, taps, after]
    aliases = {}
    if done is not None:
        aliases = {len(inputs): 0}
        specs.append(pl.BlockSpec(memory_space=pl.ANY))
        inputs.append(done)
    return pl.pallas_call(
        body,
        grid=(steps,),
        out_shape=[
            jax.ShapeDtypeStruct((rows, cols, C), BF16),
            jax.ShapeDtypeStruct((8, C), F32),
        ],
        in_specs=specs,
        out_specs=[
            pl.BlockSpec((2, cols, C), lambda g: (offset + g, 0, 0)),
            pl.BlockSpec((8, C), lambda g: (0, 0)),
        ],
        input_output_aliases=aliases,
        compiler_params=pltpu.CompilerParams(vmem_limit_bytes=10 * MIB),
        cost_estimate=pl.CostEstimate(
            flops=steps * 600_000_000, bytes_accessed=steps * 900_000, transcendentals=0
        ),
        name="conv",
    )(*inputs)


def split_kernel(keep, given, own, first, second, third):
    place = lax.axis_index("tok") // 2 % 4
    size = own.shape[0]
    for step, out in enumerate((own, first, second, third)):
        part = pl.ds(pl.multiple_of((place + step) % 4 * size, 8), size)
        out[...] = keep[part] + given[part]


def add_kernel(*refs):
    total = refs[0][...]
    for ref in refs[1:-2]:
        total = total + ref[...]
    refs[-1][...] = total


def gather_kernel(own, first, second, third, after, out):
    place = lax.axis_index("tok") // 2 % 4
    size = own.shape[0]
    for step, part in enumerate((own, first, second, third)):
        out[pl.ds(pl.multiple_of((place - step + 4) % 4 * size, 8), size)] = part[...]


def against_bank(bank, terms):
    sums = []
    for b in range(NB):
        total = terms[0] * bank[b, 0].astype(F32)
        for tap in range(1, TAPS):
            total = total + terms[tap] * bank[b, tap].astype(F32)
        sums.append(jnp.sum(total, axis=0, keepdims=True))
    return across(jnp.sum(jnp.concatenate(sums, axis=0), axis=1, keepdims=True))


def image_kernel(
    scale, images, mine, other, rows, latent, bank, style_w, select_w, target,
    after, sent, penalty, corr, proj, terms, d_scaled, d_mixed, mixed, scaled,
):
    core = lax.axis_index("tok") % 2
    half = TAPS * C // 2
    terms_flat = terms
    terms_flat[pl.ds(pl.multiple_of(core * half, 8), half)] = mine[...] * scale
    terms_flat[pl.ds(pl.multiple_of((1 - core) * half, 8), half)] = other[...] * scale
    for tap in range(TAPS):
        corr[tap] = terms_flat[tap * C : tap * C + C]
    style, demod, share = rows[0:1], rows[1:2], rows[2:3]
    style_d = down(style)
    demod3 = demod * demod * demod
    along = jnp.zeros((1, C), F32)
    for tap in range(TAPS):
        one = weighted(bank, share, tap)
        mixed[tap] = one
        one = one * style_d
        scaled[tap] = one
        along = along + jnp.sum(corr[tap] * one, axis=0, keepdims=True)
    pull = demod3 * along
    total = jnp.zeros((C, C), F32)
    work = terms.reshape(TAPS, C, C)
    for tap in range(TAPS):
        one = demod * corr[tap] - pull * scaled[tap]
        proj[tap] = one
        total = total + one * mixed[tap]
        work[tap] = one * style_d
    by_style = across(jnp.sum(total, axis=1, keepdims=True))
    by_share = against_bank(bank, work)
    inner = jnp.sum(share * by_share, axis=1, keepdims=True)
    by_logit = share * (by_share - inner)
    grad = row_dot_t(by_style, style_w[...]) + row_dot(by_logit[:, :NB], select_w[...])
    length = jnp.sqrt(jnp.sum(grad * grad, axis=1, keepdims=True) + EPS)
    gap = length - target[...]
    penalty[...] = gap * gap
    factor = (2.0 / images) * gap / length

    d_style = row_dot(grad, style_w[...])
    d_style_d = down(d_style)
    d_logit = widen(row_dot_t(grad, select_w[...]))
    mean = jnp.sum(share * d_logit, axis=1, keepdims=True)
    d_share = share * (d_logit - mean)
    cross = jnp.zeros((1, C), F32)
    turn = jnp.zeros((1, C), F32)
    for tap in range(TAPS):
        one = weighted(bank, d_share, tap)
        d_mixed[tap] = one
        one = one * style_d + mixed[tap] * d_style_d
        d_scaled[tap] = one
        cross = cross + jnp.sum(scaled[tap] * one, axis=0, keepdims=True)
        turn = turn + jnp.sum(corr[tap] * one, axis=0, keepdims=True)
    row_p = -demod * demod * cross
    row_d = -pull
    row_k = 2.0 * demod * demod * pull * cross - demod3 * turn
    total = jnp.zeros((C, C), F32)
    for tap in range(TAPS):
        one = row_p * proj[tap] + row_d * d_scaled[tap] + row_k * scaled[tap]
        total = total + one * mixed[tap] + proj[tap] * d_mixed[tap]
        work[tap] = one * style_d + proj[tap] * d_style_d
    to_style = across(jnp.sum(total, axis=1, keepdims=True))
    to_share = against_bank(bank, work) + by_share * (d_logit - mean) - d_logit * inner
    to_logit = share * (to_share - jnp.sum(share * to_share, axis=1, keepdims=True))

    last = jnp.concatenate(
        [
            x[:, :NB]
            for x in (
                factor * to_logit, by_logit, factor * share, factor * d_share, share, d_share,
            )
        ]
        + [jnp.zeros((1, C - 6 * NB), F32)],
        axis=1,
    )
    vec = latent[...]
    small = jnp.concatenate(
        [vec[:, C * j : C * j + C] for j in range(4)]
        + [factor * grad[:, C * j : C * j + C] for j in range(4)]
        + [factor * to_style, by_style, style, d_style, row_p, row_d, row_k, last],
        axis=0,
    )
    high = small.astype(BF16)
    lower = (small - high.astype(F32)).astype(BF16)
    width = C // images
    size = sent.shape[1]
    split = size // width

    def slices(taps, s):
        return jnp.concatenate([proj[tap, s * width : s * width + width] for tap in taps], axis=0)

    @pl.when(core == 0)
    def _():
        for s in range(images):
            sent[s] = slices(range(split), s).astype(BF16)

    @pl.when(core == 1)
    def _():
        none = jnp.zeros((size - 32 - (TAPS - split) * width, C), F32)
        for s in range(images):
            body = jnp.concatenate([slices(range(split, TAPS), s), none], axis=0)
            sent[s] = jnp.concatenate([high, lower, body.astype(BF16)], axis=0)


def final_kernel(
    mine, other, bank_s, bank_grad, style_grad, select_grad, got, small, flip, to_k, to_dk
):
    images, size, _ = mine.shape
    width = C // images
    split = size // width
    core = lax.axis_index("tok") % 2
    got[core] = mine[...]
    got[1 - core] = other[...]
    for n in range(images):
        small[n] = got[1, n, :16].astype(F32) + got[1, n, 16:32].astype(F32)
    styles = jnp.concatenate(
        [small[:, 10], small[:, 11], jnp.zeros((C - 2 * images, C), F32)], axis=0
    )
    flip[...] = styles.T
    shard = lax.axis_index("samp")
    style_c = flip[pl.ds(pl.multiple_of(shard * width, 8), width)]
    for n in range(images):
        last = small[n, 15:16]
        style = style_c[:, n : n + 1][None]
        d_style = style_c[:, images + n : images + n + 1][None]
        row_p, row_d, row_k = (small[n, j : j + 1][None] for j in (12, 13, 14))
        rest = got[1, n, 32:].astype(F32)[: (TAPS - split) * width]
        proj = jnp.concatenate([got[0, n].astype(F32), rest], axis=0).reshape(TAPS, width, C)
        mixed = last[:, 32:33][None] * bank_s[0]
        d_mixed = last[:, 40:41][None] * bank_s[0]
        for b in range(1, NB):
            mixed = mixed + last[:, 32 + b : 33 + b][None] * bank_s[b]
            d_mixed = d_mixed + last[:, 40 + b : 41 + b][None] * bank_s[b]
        scaled = mixed * style
        d_scaled = d_mixed * style + mixed * d_style
        second = row_p * proj + row_d * d_scaled + row_k * scaled
        to_k[n] = second * style + proj * d_style
        to_dk[n] = proj * style
    for b in range(NB):
        total = jnp.zeros((TAPS, width, C), F32)
        for n in range(images):
            last = small[n, 15:16]
            total = total + last[:, 16 + b : 17 + b][None] * to_k[n]
            total = total + last[:, 24 + b : 25 + b][None] * to_dk[n]
        bank_grad[b] = total
    last = small[:, 15]
    right = jnp.concatenate(
        [
            jnp.concatenate([small[:, 8], last], axis=1),
            jnp.concatenate([small[:, 9], pltpu.roll(last, C - NB, 1)], axis=1),
        ],
        axis=0,
    )
    for j in range(4):
        left = jnp.concatenate([small[:, j], small[:, 4 + j]], axis=0)
        both = lax.dot_general(
            left, right, (((0,), (0,)), ((), ())), precision=HIGH, preferred_element_type=F32
        )
        style_grad[C * j : C * j + C] = both[:, :C]
        select_grad[:, C * j : C * j + C] = both[:, C:].T[:NB]


def neighbour_rows(block):
    count = lax.axis_size("tok")
    core = lax.axis_index("tok") % 2
    first, last = block[:1], block[block.shape[0] - 1 :]
    swap = [(i, i ^ 1) for i in range(count)]
    pairs = [(i, i + 1) for i in range(1, count - 1, 2)]
    pairs = pairs + [(b, a) for a, b in pairs]
    far = lax.ppermute(jnp.where(core == 0, first, last), "tok", pairs)
    near = lax.ppermute(jnp.where(core == 0, last, first), "tok", swap)
    return near, far


def local(features_in, path_noise, latent, bank, style_weight, select_weight, path_mean):
    _, rows, cols, chans = features_in.shape
    images = lax.axis_size("samp")
    toks = lax.axis_size("tok")
    width = chans // images
    swap = [(i, i ^ 1) for i in range(toks)]
    scale = 1.0 / math.sqrt(rows * toks * cols)
    block, noise = features_in[0], path_noise[0]
    near, far = neighbour_rows(block)
    cube = (TAPS, C, C)
    select_t = select_weight.T
    taps, small = call(
        kernel_maker,
        [((4 * C, 6 * C), BF16), ((8, C), F32)],
        [latent, bank, style_weight, select_t],
        [pltpu.VMEM(cube, F32)],
        flops=2_000_000_000,
        name="kernel_maker",
    )
    half = TAPS * C // 2
    edge = ((3 * C, cols), BF16)
    flat, edge_low, edge_high = call(
        corr_kernel,
        [((TAPS * C, C), F32), edge, edge],
        [block, noise],
        [
            pltpu.VMEM((3 * C, 3 * C), F32),
            pltpu.VMEM(block.shape, BF16),
            pltpu.VMEM(noise.shape, BF16),
            pltpu.SemaphoreType.DMA((2, rows // GROUP)),
        ],
        flops=4_000_000_000,
        name="corr",
        far=(0, 1),
        limit=CORR_LIMIT,
    )
    keep, give = call(
        edge_kernel,
        [((half, C), F32)] * 2,
        [near, far, flat, edge_low, edge_high, small],
        [pltpu.VMEM((TAPS * C, C), F32)],
        flops=500_000_000,
        name="edge",
    )
    given = lax.ppermute(give, "tok", swap)
    quarter = ((half // 4, C), F32)

    def along_y(step):
        return [(i, i // 8 * 8 + (i + 2 * step) % 8) for i in range(toks)]

    own, *out = call(split_kernel, [quarter] * 4, [keep, given], name="split")
    features, token = conv_part(0, 3, near, far, block, taps, own, None)
    came = [lax.ppermute(x, "tok", along_y(j + 1)) for j, x in enumerate(out)]
    (own,) = call(add_kernel, [quarter], [own, *came, token], name="add_y")
    features, token = conv_part(3, 2, near, far, block, taps, own, features)
    came = lax.ppermute(own, "tok", [(i, i ^ 8) for i in range(toks)])
    (own,) = call(add_kernel, [quarter], [own, came, token], name="add_x")
    features, token = conv_part(5, 3, near, far, block, taps, own, features)
    came = [lax.ppermute(own, "tok", along_y(j)) for j in (1, 2, 3)]
    (mine,) = call(
        gather_kernel, [((half, C), F32)], [own, *came, token], name="gather_y"
    )
    other = lax.ppermute(mine, "tok", swap)
    shard = lax.axis_index("samp")
    bank_s = lax.dynamic_slice_in_dim(bank, shard * width, width, 2).astype(F32)
    message = (TAPS - 1) * width

    def image(*refs):
        image_kernel(scale, images, *refs)

    sent, penalty = call(
        image,
        [((images, message, C), BF16), ((1, 1), F32)],
        [
            mine, other, small, latent, bank, style_weight, select_t,
            path_mean.reshape(1, 1), bank_s,
        ],
        [
            pltpu.VMEM(cube, F32),
            pltpu.VMEM(cube, F32),
            pltpu.VMEM((TAPS * C, C), F32),
            pltpu.VMEM(cube, F32),
            pltpu.VMEM(cube, F32),
            pltpu.VMEM(cube, F32),
            pltpu.VMEM(cube, F32),
        ],
        flops=6_000_000_000,
        name="image",
        limit=16,
    )
    got = lax.all_to_all(sent, "samp", 0, 0)
    got_other = lax.ppermute(got, "tok", swap)
    bank_grad, style_grad, select_grad = call(
        final_kernel,
        [((NB, TAPS, width, C), F32), (style_weight.shape, F32), (select_weight.shape[::-1], F32)],
        [got, got_other, bank_s],
        [
            pltpu.VMEM((2, images, message, C), BF16),
            pltpu.VMEM((images, 16, C), F32),
            pltpu.VMEM((C, C), F32),
            pltpu.VMEM((images, TAPS, width, C), F32),
            pltpu.VMEM((images, TAPS, width, C), F32),
        ],
        name="final",
    )
    return (features[None], penalty.reshape(1), bank_grad, style_grad, select_grad.T)


def solution(mesh):
    placed = (
        P("samp", "tok", None, None),
        P("samp", "tok", None, None),
        P("samp", None),
        P(),
        P(),
        P(),
        P(),
    )
    return jax.shard_map(
        local,
        mesh=mesh,
        in_specs=placed,
        out_specs=(P("samp", "tok", None, None), P("samp"), P(None, None, "samp", None), P(), P()),
        check_vma=False,
    )
```

```python
import math

import jax
import jax.numpy as jnp
from jax import lax
from jax.experimental import pallas as pl
from jax.experimental.pallas import tpu as pltpu
from jax.sharding import PartitionSpec as P

HIGH = lax.Precision.HIGHEST
EPS = 1e-08
F32 = jnp.float32
BF16 = jnp.bfloat16
TAPS = 9
C = 128
NB = 8
GROUP = 4
CORR_LIMIT = 51
MIB = 1024 * 1024


def whole(count):
    return [pl.BlockSpec(memory_space=pltpu.VMEM)] * count


def call(kernel, outs, inputs, scratch=(), limit=10, flops=0, name=None, far=()):
    specs = whole(len(inputs))
    for place in far:
        specs[place] = pl.BlockSpec(memory_space=pltpu.HBM)
    size = sum(math.prod(x.shape) * x.dtype.itemsize for x in inputs)
    shapes = [jax.ShapeDtypeStruct(s, d) for s, d in outs]
    return pl.pallas_call(
        kernel,
        out_shape=shapes,
        in_specs=specs,
        out_specs=whole(len(outs)),
        scratch_shapes=list(scratch),
        compiler_params=pltpu.CompilerParams(vmem_limit_bytes=limit * MIB),
        cost_estimate=pl.CostEstimate(flops=flops, bytes_accessed=size, transcendentals=0),
        name=name,
    )(*inputs)


def row_dot(row, mat):
    rows = jnp.broadcast_to(row, (8, row.shape[1]))
    return jnp.dot(rows, mat, precision=HIGH, preferred_element_type=F32)[:1]


def row_dot_t(row, mat):
    rows = jnp.broadcast_to(row, (8, row.shape[1]))
    return lax.dot_general(
        rows, mat, (((1,), (1,)), ((), ())), precision=HIGH, preferred_element_type=F32
    )[:1]


def down(row):
    return jnp.broadcast_to(row, (C, C)).T


def across(col):
    size = col.shape[0]
    lane = lax.broadcasted_iota(jnp.int32, (size, C), 1)
    line = lax.broadcasted_iota(jnp.int32, (size, C), 0)
    return jnp.sum(jnp.where(lane == line, col, 0.0), axis=0, keepdims=True)


def widen(row):
    return jnp.concatenate([row, jnp.zeros((1, C - row.shape[1]), F32)], axis=1)


def weighted(bank, weights, tap):
    total = weights[:, 0:1] * bank[0, tap].astype(F32)
    for b in range(1, NB):
        total = total + weights[:, b : b + 1] * bank[b, tap].astype(F32)
    return total


def kernel_maker(latent, bank, style_w, select_w, taps, rows, scaled):
    vec = latent[...]
    expo = jnp.exp(row_dot_t(vec, select_w[...]))
    share = expo / jnp.sum(expo, axis=1, keepdims=True)
    style = row_dot(vec, style_w[...]) + 1.0
    style_d = down(style)
    power = jnp.zeros((1, C), F32)
    for tap in range(TAPS):
        one = weighted(bank, share, tap) * style_d
        scaled[tap] = one
        power = power + jnp.sum(one * one, axis=0, keepdims=True)
    demod = lax.rsqrt(power + EPS)
    zero = jnp.zeros((C, C), BF16)
    for line in range(4):
        for out in range(2):
            for kx in range(3):
                ky = line - out
                at = (3 * out + kx) * C
                if 0 <= ky < 3:
                    block = (scaled[3 * ky + kx] * demod).astype(BF16)
                else:
                    block = zero
                taps[line * C : line * C + C, at : at + C] = block
    rows[0:1] = style
    rows[1:2] = demod
    rows[2:3] = widen(share)
    rows[3:8] = jnp.zeros((5, C), F32)


def corr_kernel(block_far, noise_far, flat, edge_low, edge_high, acc, block, noise, sems):
    height, width, _ = block.shape
    group = GROUP
    count = height // group

    def fetch(which, index):
        source, target = ((block_far, block), (noise_far, noise))[which]
        part = pl.ds(index * group, group)
        return pltpu.make_async_copy(source.at[part], target.at[part], sems.at[which, index])

    fetch(0, 0).start()
    for index in range(count):
        if index + 1 < count:
            fetch(0, index + 1).start()
        fetch(1, index).start()
    fetch(0, 0).wait()
    acc[...] = jnp.zeros_like(acc)
    lane = lax.broadcasted_iota(jnp.int32, (C, group * width), 1) % width

    def ready(index):
        if index + 1 < count:
            fetch(0, index + 1).wait()
        fetch(1, index).wait()

    def step(start, above, here, below):
        side = noise[pl.ds(start, group)].reshape(group * width, C).T
        zero = jnp.zeros_like(side)
        later = jnp.where(lane == width - 1, zero, pltpu.roll(side, group * width - 1, 1))
        former = jnp.where(lane == 0, zero, pltpu.roll(side, 1, 1))
        left = jnp.concatenate([later, side, former], axis=0)
        right = jnp.concatenate([above, here, below], axis=1)
        acc[...] += jnp.dot(left, right, preferred_element_type=F32)
        return left

    def lines(start):
        return block[pl.ds(start, group)].reshape(group * width, C)

    rest = (group - 1) * width
    none = jnp.zeros((width, C), BF16)
    ready(0)
    left = step(
        0,
        jnp.concatenate([none, block[0 : group - 1].reshape(rest, C)], axis=0),
        lines(0),
        lines(1),
    )
    edge_low[...] = left[:, :width]

    for index in range(1, count - 1):
        ready(index)
        start = index * group
        step(start, lines(start - 1), lines(start), lines(start + 1))

    start = height - group
    ready(count - 1)
    left = step(
        start,
        lines(start - 1),
        lines(start),
        jnp.concatenate([block[start + 1 : height].reshape(rest, C), none], axis=0),
    )
    edge_high[...] = left[:, rest:]
    for ky in range(3):
        for kx in range(3):
            tap = 3 * ky + kx
            flat[tap * C : tap * C + C] = acc[kx * C : kx * C + C, ky * C : ky * C + C].T


def edge_kernel(near, far, flat, edge_low, edge_high, keep, give, both):
    core = lax.axis_index("tok") % 2
    first = jnp.where(core == 0, far[0], near[0])
    last = jnp.where(core == 0, near[0], far[0])
    above = jnp.dot(edge_low[...], first, preferred_element_type=F32)
    below = jnp.dot(edge_high[...], last, preferred_element_type=F32)
    side = 3 * C
    both[side : 2 * side] = flat[side : 2 * side]
    for kx in range(3):
        at = kx * C
        both[at : at + C] = flat[at : at + C] + above[at : at + C].T
        low = 2 * side + at
        both[low : low + C] = flat[low : low + C] + below[at : at + C].T
    half = TAPS * C // 2
    keep[...] = both[pl.ds(pl.multiple_of(core * half, 8), half)]
    give[...] = both[pl.ds(pl.multiple_of((1 - core) * half, 8), half)]


def conv_kernel(offset, pairs, final, near, far, above, lines, below, taps, *rest):
    out, token = rest[-2:]
    token[...] = jnp.zeros_like(token)
    width = lines.shape[1]
    line = lax.broadcasted_iota(jnp.int32, (width, C), 0)
    core = lax.axis_index("tok") % 2
    place = offset + pl.program_id(0)
    first, last = above[0], below[0]
    if offset == 0:
        first = jnp.where(place == 0, jnp.where(core == 0, far[0], near[0]), first)
    if final:
        last = jnp.where(place == pairs - 1, jnp.where(core == 0, near[0], far[0]), last)
    left = jnp.concatenate([first, lines[0], lines[1], last], axis=1)
    both = jnp.dot(left, taps[...], preferred_element_type=F32)
    for j in range(2):
        part = both[:, 3 * C * j : 3 * C * j + 3 * C]
        former = jnp.where(line == 0, 0.0, pltpu.roll(part[:, :C], 1, 0))
        later = jnp.where(line == width - 1, 0.0, pltpu.roll(part[:, 2 * C :], width - 1, 0))
        out[j] = (former + part[:, C : 2 * C] + later).astype(BF16)


def conv_part(offset, steps, near, far, block, taps, after, done):
    rows, cols, _ = block.shape
    pairs = rows // 2
    one = (1, cols, C)

    def body(*refs):
        conv_kernel(offset, pairs, offset + steps == pairs, *refs)

    specs = [
        pl.BlockSpec(one, lambda g: (0, 0, 0)),
        pl.BlockSpec(one, lambda g: (0, 0, 0)),
        pl.BlockSpec(one, lambda g: (jnp.maximum(2 * (offset + g) - 1, 0), 0, 0)),
        pl.BlockSpec((2, cols, C), lambda g: (offset + g, 0, 0)),
        pl.BlockSpec(one, lambda g: (jnp.minimum(2 * (offset + g) + 2, rows - 1), 0, 0)),
        pl.BlockSpec(taps.shape, lambda g: (0, 0)),
        pl.BlockSpec(memory_space=pl.ANY),
    ]
    inputs = [near, far, block, block, block, taps, after]
    aliases = {}
    if done is not None:
        aliases = {len(inputs): 0}
        specs.append(pl.BlockSpec(memory_space=pl.ANY))
        inputs.append(done)
    return pl.pallas_call(
        body,
        grid=(steps,),
        out_shape=[
            jax.ShapeDtypeStruct((rows, cols, C), BF16),
            jax.ShapeDtypeStruct((8, C), F32),
        ],
        in_specs=specs,
        out_specs=[
            pl.BlockSpec((2, cols, C), lambda g: (offset + g, 0, 0)),
            pl.BlockSpec((8, C), lambda g: (0, 0)),
        ],
        input_output_aliases=aliases,
        compiler_params=pltpu.CompilerParams(vmem_limit_bytes=10 * MIB),
        cost_estimate=pl.CostEstimate(
            flops=steps * 600_000_000, bytes_accessed=steps * 900_000, transcendentals=0
        ),
        name="conv",
    )(*inputs)


def split_kernel(keep, given, rows, own, first, second, third):
    place = lax.axis_index("tok") // 2 % 4
    size = own.shape[0]
    for step, out in enumerate((own, first, second, third)):
        part = pl.ds(pl.multiple_of((place + step) % 4 * size, 8), size)
        out[...] = keep[part] + given[part]


def add_kernel(*refs):
    total = refs[0][...]
    for ref in refs[1:-2]:
        total = total + ref[...]
    refs[-1][...] = total


def gather_kernel(own, first, second, third, after, out):
    place = lax.axis_index("tok") // 2 % 4
    size = own.shape[0]
    for step, part in enumerate((own, first, second, third)):
        out[pl.ds(pl.multiple_of((place - step + 4) % 4 * size, 8), size)] = part[...]


def against_bank(bank, terms):
    sums = []
    for b in range(NB):
        total = terms[0] * bank[b, 0].astype(F32)
        for tap in range(1, TAPS):
            total = total + terms[tap] * bank[b, tap].astype(F32)
        sums.append(jnp.sum(total, axis=0, keepdims=True))
    return across(jnp.sum(jnp.concatenate(sums, axis=0), axis=1, keepdims=True))


def image_kernel(
    scale, images, mine, other, rows, latent, bank, style_w, select_w, target,
    after, sent, penalty, corr, proj, terms, d_scaled, d_mixed, mixed, scaled,
):
    core = lax.axis_index("tok") % 2
    half = TAPS * C // 2
    terms_flat = terms
    terms_flat[pl.ds(pl.multiple_of(core * half, 8), half)] = mine[...] * scale
    terms_flat[pl.ds(pl.multiple_of((1 - core) * half, 8), half)] = other[...] * scale
    for tap in range(TAPS):
        corr[tap] = terms_flat[tap * C : tap * C + C]
    style, demod, share = rows[0:1], rows[1:2], rows[2:3]
    style_d = down(style)
    demod3 = demod * demod * demod
    along = jnp.zeros((1, C), F32)
    for tap in range(TAPS):
        one = weighted(bank, share, tap)
        mixed[tap] = one
        one = one * style_d
        scaled[tap] = one
        along = along + jnp.sum(corr[tap] * one, axis=0, keepdims=True)
    pull = demod3 * along
    total = jnp.zeros((C, C), F32)
    work = terms.reshape(TAPS, C, C)
    for tap in range(TAPS):
        one = demod * corr[tap] - pull * scaled[tap]
        proj[tap] = one
        total = total + one * mixed[tap]
        work[tap] = one * style_d
    by_style = across(jnp.sum(total, axis=1, keepdims=True))
    by_share = against_bank(bank, work)
    inner = jnp.sum(share * by_share, axis=1, keepdims=True)
    by_logit = share * (by_share - inner)
    grad = row_dot_t(by_style, style_w[...]) + row_dot(by_logit[:, :NB], select_w[...])
    length = jnp.sqrt(jnp.sum(grad * grad, axis=1, keepdims=True) + EPS)
    gap = length - target[...]
    penalty[...] = gap * gap
    factor = (2.0 / images) * gap / length

    d_style = row_dot(grad, style_w[...])
    d_style_d = down(d_style)
    d_logit = widen(row_dot_t(grad, select_w[...]))
    mean = jnp.sum(share * d_logit, axis=1, keepdims=True)
    d_share = share * (d_logit - mean)
    cross = jnp.zeros((1, C), F32)
    turn = jnp.zeros((1, C), F32)
    for tap in range(TAPS):
        one = weighted(bank, d_share, tap)
        d_mixed[tap] = one
        one = one * style_d + mixed[tap] * d_style_d
        d_scaled[tap] = one
        cross = cross + jnp.sum(scaled[tap] * one, axis=0, keepdims=True)
        turn = turn + jnp.sum(corr[tap] * one, axis=0, keepdims=True)
    row_p = -demod * demod * cross
    row_d = -pull
    row_k = 2.0 * demod * demod * pull * cross - demod3 * turn
    total = jnp.zeros((C, C), F32)
    for tap in range(TAPS):
        one = row_p * proj[tap] + row_d * d_scaled[tap] + row_k * scaled[tap]
        total = total + one * mixed[tap] + proj[tap] * d_mixed[tap]
        work[tap] = one * style_d + proj[tap] * d_style_d
    to_style = across(jnp.sum(total, axis=1, keepdims=True))
    to_share = against_bank(bank, work) + by_share * (d_logit - mean) - d_logit * inner
    to_logit = share * (to_share - jnp.sum(share * to_share, axis=1, keepdims=True))

    last = jnp.concatenate(
        [
            x[:, :NB]
            for x in (
                factor * to_logit, by_logit, factor * share, factor * d_share, share, d_share,
            )
        ]
        + [jnp.zeros((1, C - 6 * NB), F32)],
        axis=1,
    )
    vec = latent[...]
    small = jnp.concatenate(
        [vec[:, C * j : C * j + C] for j in range(4)]
        + [factor * grad[:, C * j : C * j + C] for j in range(4)]
        + [factor * to_style, by_style, style, d_style, row_p, row_d, row_k, last],
        axis=0,
    )
    high = small.astype(BF16)
    lower = (small - high.astype(F32)).astype(BF16)
    width = C // images
    size = sent.shape[1]
    split = size // width

    def slices(taps, s):
        return jnp.concatenate([proj[tap, s * width : s * width + width] for tap in taps], axis=0)

    @pl.when(core == 0)
    def _():
        for s in range(images):
            sent[s] = slices(range(split), s).astype(BF16)

    @pl.when(core == 1)
    def _():
        none = jnp.zeros((size - 32 - (TAPS - split) * width, C), F32)
        for s in range(images):
            body = jnp.concatenate([slices(range(split, TAPS), s), none], axis=0)
            sent[s] = jnp.concatenate([high, lower, body.astype(BF16)], axis=0)


def final_kernel(
    mine, other, bank_s, bank_grad, style_grad, select_grad, got, small, flip, to_k, to_dk
):
    images, size, _ = mine.shape
    width = C // images
    split = size // width
    core = lax.axis_index("tok") % 2
    got[core] = mine[...]
    got[1 - core] = other[...]
    for n in range(images):
        small[n] = got[1, n, :16].astype(F32) + got[1, n, 16:32].astype(F32)
    styles = jnp.concatenate(
        [small[:, 10], small[:, 11], jnp.zeros((C - 2 * images, C), F32)], axis=0
    )
    flip[...] = styles.T
    shard = lax.axis_index("samp")
    style_c = flip[pl.ds(pl.multiple_of(shard * width, 8), width)]
    for n in range(images):
        last = small[n, 15:16]
        style = style_c[:, n : n + 1][None]
        d_style = style_c[:, images + n : images + n + 1][None]
        row_p, row_d, row_k = (small[n, j : j + 1][None] for j in (12, 13, 14))
        rest = got[1, n, 32:].astype(F32)[: (TAPS - split) * width]
        proj = jnp.concatenate([got[0, n].astype(F32), rest], axis=0).reshape(TAPS, width, C)
        mixed = last[:, 32:33][None] * bank_s[0]
        d_mixed = last[:, 40:41][None] * bank_s[0]
        for b in range(1, NB):
            mixed = mixed + last[:, 32 + b : 33 + b][None] * bank_s[b]
            d_mixed = d_mixed + last[:, 40 + b : 41 + b][None] * bank_s[b]
        scaled = mixed * style
        d_scaled = d_mixed * style + mixed * d_style
        second = row_p * proj + row_d * d_scaled + row_k * scaled
        to_k[n] = second * style + proj * d_style
        to_dk[n] = proj * style
    for b in range(NB):
        total = jnp.zeros((TAPS, width, C), F32)
        for n in range(images):
            last = small[n, 15:16]
            total = total + last[:, 16 + b : 17 + b][None] * to_k[n]
            total = total + last[:, 24 + b : 25 + b][None] * to_dk[n]
        bank_grad[b] = total
    last = small[:, 15]
    right = jnp.concatenate(
        [
            jnp.concatenate([small[:, 8], last], axis=1),
            jnp.concatenate([small[:, 9], pltpu.roll(last, C - NB, 1)], axis=1),
        ],
        axis=0,
    )
    for j in range(4):
        left = jnp.concatenate([small[:, j], small[:, 4 + j]], axis=0)
        both = lax.dot_general(
            left, right, (((0,), (0,)), ((), ())), precision=HIGH, preferred_element_type=F32
        )
        style_grad[C * j : C * j + C] = both[:, :C]
        select_grad[:, C * j : C * j + C] = both[:, C:].T[:NB]


def neighbour_rows(block):
    count = lax.axis_size("tok")
    core = lax.axis_index("tok") % 2
    first, last = block[:1], block[block.shape[0] - 1 :]
    swap = [(i, i ^ 1) for i in range(count)]
    pairs = [(i, i + 1) for i in range(1, count - 1, 2)]
    pairs = pairs + [(b, a) for a, b in pairs]
    far = lax.ppermute(jnp.where(core == 0, first, last), "tok", pairs)
    near = lax.ppermute(jnp.where(core == 0, last, first), "tok", swap)
    return near, far


def local(features_in, path_noise, latent, bank, style_weight, select_weight, path_mean):
    _, rows, cols, chans = features_in.shape
    images = lax.axis_size("samp")
    toks = lax.axis_size("tok")
    width = chans // images
    swap = [(i, i ^ 1) for i in range(toks)]
    scale = 1.0 / math.sqrt(rows * toks * cols)
    block, noise = features_in[0], path_noise[0]
    near, far = neighbour_rows(block)
    cube = (TAPS, C, C)
    select_t = select_weight.T
    taps, small = call(
        kernel_maker,
        [((4 * C, 6 * C), BF16), ((8, C), F32)],
        [latent, bank, style_weight, select_t],
        [pltpu.VMEM(cube, F32)],
        flops=2_000_000_000,
        name="kernel_maker",
    )
    half = TAPS * C // 2
    edge = ((3 * C, cols), BF16)
    flat, edge_low, edge_high = call(
        corr_kernel,
        [((TAPS * C, C), F32), edge, edge],
        [block, noise],
        [
            pltpu.VMEM((3 * C, 3 * C), F32),
            pltpu.VMEM(block.shape, BF16),
            pltpu.VMEM(noise.shape, BF16),
            pltpu.SemaphoreType.DMA((2, rows // GROUP)),
        ],
        flops=4_000_000_000,
        name="corr",
        far=(0, 1),
        limit=CORR_LIMIT,
    )
    keep, give = call(
        edge_kernel,
        [((half, C), F32)] * 2,
        [near, far, flat, edge_low, edge_high],
        [pltpu.VMEM((TAPS * C, C), F32)],
        flops=500_000_000,
        name="edge",
    )
    given = lax.ppermute(give, "tok", swap)
    quarter = ((half // 4, C), F32)

    def along_y(step):
        return [(i, i // 8 * 8 + (i + 2 * step) % 8) for i in range(toks)]

    own, *out = call(split_kernel, [quarter] * 4, [keep, given, small], name="split")
    features, token = conv_part(0, 3, near, far, block, taps, own, None)
    came = [lax.ppermute(out[j - 1], "tok", along_y(j)) for j in (2, 1, 3)]
    (own,) = call(add_kernel, [quarter], [own, *came, token], name="add_y")
    features, token = conv_part(3, 2, near, far, block, taps, own, features)
    came = lax.ppermute(own, "tok", [(i, i ^ 8) for i in range(toks)])
    (own,) = call(add_kernel, [quarter], [own, came, token], name="add_x")
    features, token = conv_part(5, 3, near, far, block, taps, own, features)
    came = [lax.ppermute(own, "tok", along_y(j)) for j in (2, 1, 3)]
    came = [came[1], came[0], came[2]]
    (mine,) = call(
        gather_kernel, [((half, C), F32)], [own, *came, token], name="gather_y"
    )
    other = lax.ppermute(mine, "tok", swap)
    shard = lax.axis_index("samp")
    bank_s = lax.dynamic_slice_in_dim(bank, shard * width, width, 2).astype(F32)
    message = (TAPS - 1) * width

    def image(*refs):
        image_kernel(scale, images, *refs)

    sent, penalty = call(
        image,
        [((images, message, C), BF16), ((1, 1), F32)],
        [
            mine, other, small, latent, bank, style_weight, select_t,
            path_mean.reshape(1, 1), bank_s,
        ],
        [
            pltpu.VMEM(cube, F32),
            pltpu.VMEM(cube, F32),
            pltpu.VMEM((TAPS * C, C), F32),
            pltpu.VMEM(cube, F32),
            pltpu.VMEM(cube, F32),
            pltpu.VMEM(cube, F32),
            pltpu.VMEM(cube, F32),
        ],
        flops=6_000_000_000,
        name="image",
        limit=16,
    )
    got = lax.all_to_all(sent, "samp", 0, 0)
    got_other = lax.ppermute(got, "tok", swap)
    bank_grad, style_grad, select_grad = call(
        final_kernel,
        [((NB, TAPS, width, C), F32), (style_weight.shape, F32), (select_weight.shape[::-1], F32)],
        [got, got_other, bank_s],
        [
            pltpu.VMEM((2, images, message, C), BF16),
            pltpu.VMEM((images, 16, C), F32),
            pltpu.VMEM((C, C), F32),
            pltpu.VMEM((images, TAPS, width, C), F32),
            pltpu.VMEM((images, TAPS, width, C), F32),
        ],
        name="final",
    )
    return (features[None], penalty.reshape(1), bank_grad, style_grad, select_grad.T)


def solution(mesh):
    placed = (
        P("samp", "tok", None, None),
        P("samp", "tok", None, None),
        P("samp", None),
        P(),
        P(),
        P(),
        P(),
    )
    return jax.shard_map(
        local,
        mesh=mesh,
        in_specs=placed,
        out_specs=(P("samp", "tok", None, None), P("samp"), P(None, None, "samp", None), P(), P()),
        check_vma=False,
    )
```

```python
import math

import jax
import jax.numpy as jnp
from jax import lax
from jax.experimental import pallas as pl
from jax.experimental.pallas import tpu as pltpu
from jax.sharding import PartitionSpec as P

HIGH = lax.Precision.HIGHEST
EPS = 1e-08
F32 = jnp.float32
BF16 = jnp.bfloat16
TAPS = 9
C = 128
NB = 8
GROUP = 8
CORR_LIMIT = 51
MIB = 1024 * 1024


def whole(count):
    return [pl.BlockSpec(memory_space=pltpu.VMEM)] * count


def call(kernel, outs, inputs, scratch=(), limit=10, flops=0, name=None, far=()):
    specs = whole(len(inputs))
    for place in far:
        specs[place] = pl.BlockSpec(memory_space=pltpu.HBM)
    size = sum(math.prod(x.shape) * x.dtype.itemsize for x in inputs)
    shapes = [jax.ShapeDtypeStruct(s, d) for s, d in outs]
    return pl.pallas_call(
        kernel,
        out_shape=shapes,
        in_specs=specs,
        out_specs=whole(len(outs)),
        scratch_shapes=list(scratch),
        compiler_params=pltpu.CompilerParams(vmem_limit_bytes=limit * MIB),
        cost_estimate=pl.CostEstimate(flops=flops, bytes_accessed=size, transcendentals=0),
        name=name,
    )(*inputs)


def row_dot(row, mat):
    rows = jnp.broadcast_to(row, (8, row.shape[1]))
    return jnp.dot(rows, mat, precision=HIGH, preferred_element_type=F32)[:1]


def row_dot_t(row, mat):
    rows = jnp.broadcast_to(row, (8, row.shape[1]))
    return lax.dot_general(
        rows, mat, (((1,), (1,)), ((), ())), precision=HIGH, preferred_element_type=F32
    )[:1]


def down(row):
    return jnp.broadcast_to(row, (C, C)).T


def across(col):
    size = col.shape[0]
    lane = lax.broadcasted_iota(jnp.int32, (size, C), 1)
    line = lax.broadcasted_iota(jnp.int32, (size, C), 0)
    return jnp.sum(jnp.where(lane == line, col, 0.0), axis=0, keepdims=True)


def widen(row):
    return jnp.concatenate([row, jnp.zeros((1, C - row.shape[1]), F32)], axis=1)


def weighted(bank, weights, tap):
    total = weights[:, 0:1] * bank[0, tap].astype(F32)
    for b in range(1, NB):
        total = total + weights[:, b : b + 1] * bank[b, tap].astype(F32)
    return total


def kernel_maker(latent, bank, style_w, select_w, taps, rows, scaled):
    vec = latent[...]
    expo = jnp.exp(row_dot_t(vec, select_w[...]))
    share = expo / jnp.sum(expo, axis=1, keepdims=True)
    style = row_dot(vec, style_w[...]) + 1.0
    style_d = down(style)
    power = jnp.zeros((1, C), F32)
    for tap in range(TAPS):
        one = weighted(bank, share, tap) * style_d
        scaled[tap] = one
        power = power + jnp.sum(one * one, axis=0, keepdims=True)
    demod = lax.rsqrt(power + EPS)
    zero = jnp.zeros((C, C), BF16)
    for line in range(4):
        for out in range(2):
            for kx in range(3):
                ky = line - out
                at = (3 * out + kx) * C
                if 0 <= ky < 3:
                    block = (scaled[3 * ky + kx] * demod).astype(BF16)
                else:
                    block = zero
                taps[line * C : line * C + C, at : at + C] = block
    rows[0:1] = style
    rows[1:2] = demod
    rows[2:3] = widen(share)
    rows[3:8] = jnp.zeros((5, C), F32)


def corr_kernel(block_far, noise_far, flat, edge_low, edge_high, acc, block, noise, sems):
    height, width, _ = block.shape
    group = GROUP
    count = height // group

    def fetch(which, index):
        source, target = ((block_far, block), (noise_far, noise))[which]
        part = pl.ds(index * group, group)
        return pltpu.make_async_copy(source.at[part], target.at[part], sems.at[which, index])

    fetch(0, 0).start()
    for index in range(count):
        if index + 1 < count:
            fetch(0, index + 1).start()
        fetch(1, index).start()
    fetch(0, 0).wait()
    acc[...] = jnp.zeros_like(acc)
    lane = lax.broadcasted_iota(jnp.int32, (C, group * width), 1) % width

    def ready(index):
        if index + 1 < count:
            fetch(0, index + 1).wait()
        fetch(1, index).wait()

    def step(start, above, here, below):
        side = noise[pl.ds(start, group)].reshape(group * width, C).T
        zero = jnp.zeros_like(side)
        later = jnp.where(lane == width - 1, zero, pltpu.roll(side, group * width - 1, 1))
        former = jnp.where(lane == 0, zero, pltpu.roll(side, 1, 1))
        left = jnp.concatenate([later, side, former], axis=0)
        right = jnp.concatenate([above, here, below], axis=1)
        acc[...] += jnp.dot(left, right, preferred_element_type=F32)
        return left

    def lines(start):
        return block[pl.ds(start, group)].reshape(group * width, C)

    rest = (group - 1) * width
    none = jnp.zeros((width, C), BF16)
    ready(0)
    left = step(
        0,
        jnp.concatenate([none, block[0 : group - 1].reshape(rest, C)], axis=0),
        lines(0),
        lines(1),
    )
    edge_low[...] = left[:, :width]

    for index in range(1, count - 1):
        ready(index)
        start = index * group
        step(start, lines(start - 1), lines(start), lines(start + 1))

    start = height - group
    ready(count - 1)
    left = step(
        start,
        lines(start - 1),
        lines(start),
        jnp.concatenate([block[start + 1 : height].reshape(rest, C), none], axis=0),
    )
    edge_high[...] = left[:, rest:]
    for ky in range(3):
        for kx in range(3):
            tap = 3 * ky + kx
            flat[tap * C : tap * C + C] = acc[kx * C : kx * C + C, ky * C : ky * C + C].T


def edge_kernel(near, far, flat, edge_low, edge_high, keep, give, both):
    core = lax.axis_index("tok") % 2
    first = jnp.where(core == 0, far[0], near[0])
    last = jnp.where(core == 0, near[0], far[0])
    above = jnp.dot(edge_low[...], first, preferred_element_type=F32)
    below = jnp.dot(edge_high[...], last, preferred_element_type=F32)
    side = 3 * C
    both[side : 2 * side] = flat[side : 2 * side]
    for kx in range(3):
        at = kx * C
        both[at : at + C] = flat[at : at + C] + above[at : at + C].T
        low = 2 * side + at
        both[low : low + C] = flat[low : low + C] + below[at : at + C].T
    half = TAPS * C // 2
    keep[...] = both[pl.ds(pl.multiple_of(core * half, 8), half)]
    give[...] = both[pl.ds(pl.multiple_of((1 - core) * half, 8), half)]


def conv_kernel(offset, pairs, final, near, far, above, lines, below, taps, *rest):
    out, token = rest[-2:]
    token[...] = jnp.zeros_like(token)
    width = lines.shape[1]
    line = lax.broadcasted_iota(jnp.int32, (width, C), 0)
    core = lax.axis_index("tok") % 2
    place = offset + pl.program_id(0)
    first, last = above[0], below[0]
    if offset == 0:
        first = jnp.where(place == 0, jnp.where(core == 0, far[0], near[0]), first)
    if final:
        last = jnp.where(place == pairs - 1, jnp.where(core == 0, near[0], far[0]), last)
    left = jnp.concatenate([first, lines[0], lines[1], last], axis=1)
    both = jnp.dot(left, taps[...], preferred_element_type=F32)
    for j in range(2):
        part = both[:, 3 * C * j : 3 * C * j + 3 * C]
        former = jnp.where(line == 0, 0.0, pltpu.roll(part[:, :C], 1, 0))
        later = jnp.where(line == width - 1, 0.0, pltpu.roll(part[:, 2 * C :], width - 1, 0))
        out[j] = (former + part[:, C : 2 * C] + later).astype(BF16)


def conv_part(offset, steps, near, far, block, taps, after, done):
    rows, cols, _ = block.shape
    pairs = rows // 2
    one = (1, cols, C)

    def body(*refs):
        conv_kernel(offset, pairs, offset + steps == pairs, *refs)

    specs = [
        pl.BlockSpec(one, lambda g: (0, 0, 0)),
        pl.BlockSpec(one, lambda g: (0, 0, 0)),
        pl.BlockSpec(one, lambda g: (jnp.maximum(2 * (offset + g) - 1, 0), 0, 0)),
        pl.BlockSpec((2, cols, C), lambda g: (offset + g, 0, 0)),
        pl.BlockSpec(one, lambda g: (jnp.minimum(2 * (offset + g) + 2, rows - 1), 0, 0)),
        pl.BlockSpec(taps.shape, lambda g: (0, 0)),
        pl.BlockSpec(memory_space=pl.ANY),
    ]
    inputs = [near, far, block, block, block, taps, after]
    aliases = {}
    if done is not None:
        aliases = {len(inputs): 0}
        specs.append(pl.BlockSpec(memory_space=pl.ANY))
        inputs.append(done)
    return pl.pallas_call(
        body,
        grid=(steps,),
        out_shape=[
            jax.ShapeDtypeStruct((rows, cols, C), BF16),
            jax.ShapeDtypeStruct((8, C), F32),
        ],
        in_specs=specs,
        out_specs=[
            pl.BlockSpec((2, cols, C), lambda g: (offset + g, 0, 0)),
            pl.BlockSpec((8, C), lambda g: (0, 0)),
        ],
        input_output_aliases=aliases,
        compiler_params=pltpu.CompilerParams(vmem_limit_bytes=10 * MIB),
        cost_estimate=pl.CostEstimate(
            flops=steps * 600_000_000, bytes_accessed=steps * 900_000, transcendentals=0
        ),
        name="conv",
    )(*inputs)


def split_kernel(keep, given, rows, own, first, second, third):
    place = lax.axis_index("tok") // 2 % 4
    size = own.shape[0]
    for step, out in enumerate((own, first, second, third)):
        part = pl.ds(pl.multiple_of((place + step) % 4 * size, 8), size)
        out[...] = keep[part] + given[part]


def add_kernel(*refs):
    total = refs[0][...]
    for ref in refs[1:-2]:
        total = total + ref[...]
    refs[-1][...] = total


def gather_kernel(own, first, second, third, after, out):
    place = lax.axis_index("tok") // 2 % 4
    size = own.shape[0]
    for step, part in enumerate((own, first, second, third)):
        out[pl.ds(pl.multiple_of((place - step + 4) % 4 * size, 8), size)] = part[...]


def against_bank(bank, terms):
    sums = []
    for b in range(NB):
        total = terms[0] * bank[b, 0].astype(F32)
        for tap in range(1, TAPS):
            total = total + terms[tap] * bank[b, tap].astype(F32)
        sums.append(jnp.sum(total, axis=0, keepdims=True))
    return across(jnp.sum(jnp.concatenate(sums, axis=0), axis=1, keepdims=True))


def image_kernel(
    scale, images, mine, other, rows, latent, bank, style_w, select_w, target,
    after, sent, penalty, corr, proj, terms, d_scaled, d_mixed, mixed, scaled,
):
    core = lax.axis_index("tok") % 2
    half = TAPS * C // 2
    flat = corr.reshape(TAPS * C, C)
    flat[pl.ds(pl.multiple_of(core * half, 8), half)] = mine[...] * scale
    flat[pl.ds(pl.multiple_of((1 - core) * half, 8), half)] = other[...] * scale
    style, demod, share = rows[0:1], rows[1:2], rows[2:3]
    style_d = down(style)
    demod3 = demod * demod * demod
    along = jnp.zeros((1, C), F32)
    for tap in range(TAPS):
        one = weighted(bank, share, tap)
        mixed[tap] = one
        one = one * style_d
        scaled[tap] = one
        along = along + jnp.sum(corr[tap] * one, axis=0, keepdims=True)
    pull = demod3 * along
    total = jnp.zeros((C, C), F32)
    work = terms.reshape(TAPS, C, C)
    for tap in range(TAPS):
        one = demod * corr[tap] - pull * scaled[tap]
        proj[tap] = one
        total = total + one * mixed[tap]
        work[tap] = one * style_d
    by_style = across(jnp.sum(total, axis=1, keepdims=True))
    by_share = against_bank(bank, work)
    inner = jnp.sum(share * by_share, axis=1, keepdims=True)
    by_logit = share * (by_share - inner)
    grad = row_dot_t(by_style, style_w[...]) + row_dot(by_logit[:, :NB], select_w[...])
    length = jnp.sqrt(jnp.sum(grad * grad, axis=1, keepdims=True) + EPS)
    gap = length - target[...]
    penalty[...] = gap * gap
    factor = (2.0 / images) * gap / length

    d_style = row_dot(grad, style_w[...])
    d_style_d = down(d_style)
    d_logit = widen(row_dot_t(grad, select_w[...]))
    mean = jnp.sum(share * d_logit, axis=1, keepdims=True)
    d_share = share * (d_logit - mean)
    cross = jnp.zeros((1, C), F32)
    turn = jnp.zeros((1, C), F32)
    for tap in range(TAPS):
        one = weighted(bank, d_share, tap)
        d_mixed[tap] = one
        one = one * style_d + mixed[tap] * d_style_d
        d_scaled[tap] = one
        cross = cross + jnp.sum(scaled[tap] * one, axis=0, keepdims=True)
        turn = turn + jnp.sum(corr[tap] * one, axis=0, keepdims=True)
    row_p = -demod * demod * cross
    row_d = -pull
    row_k = 2.0 * demod * demod * pull * cross - demod3 * turn
    total = jnp.zeros((C, C), F32)
    for tap in range(TAPS):
        one = row_p * proj[tap] + row_d * d_scaled[tap] + row_k * scaled[tap]
        total = total + one * mixed[tap] + proj[tap] * d_mixed[tap]
        work[tap] = one * style_d + proj[tap] * d_style_d
    to_style = across(jnp.sum(total, axis=1, keepdims=True))
    to_share = against_bank(bank, work) + by_share * (d_logit - mean) - d_logit * inner
    to_logit = share * (to_share - jnp.sum(share * to_share, axis=1, keepdims=True))

    last = jnp.concatenate(
        [
            x[:, :NB]
            for x in (
                factor * to_logit, by_logit, factor * share, factor * d_share, share, d_share,
            )
        ]
        + [jnp.zeros((1, C - 6 * NB), F32)],
        axis=1,
    )
    vec = latent[...]
    small = jnp.concatenate(
        [vec[:, C * j : C * j + C] for j in range(4)]
        + [factor * grad[:, C * j : C * j + C] for j in range(4)]
        + [factor * to_style, by_style, style, d_style, row_p, row_d, row_k, last],
        axis=0,
    )
    high = small.astype(BF16)
    lower = (small - high.astype(F32)).astype(BF16)
    width = C // images
    size = sent.shape[1]
    split = size // width

    def slices(taps, s):
        return jnp.concatenate([proj[tap, s * width : s * width + width] for tap in taps], axis=0)

    @pl.when(core == 0)
    def _():
        for s in range(images):
            sent[s] = slices(range(split), s).astype(BF16)

    @pl.when(core == 1)
    def _():
        none = jnp.zeros((size - 32 - (TAPS - split) * width, C), F32)
        for s in range(images):
            body = jnp.concatenate([slices(range(split, TAPS), s), none], axis=0)
            sent[s] = jnp.concatenate([high, lower, body.astype(BF16)], axis=0)


def final_kernel(
    mine, other, bank_s, bank_grad, style_grad, select_grad, got, small, flip, to_k, to_dk
):
    images, size, _ = mine.shape
    width = C // images
    split = size // width
    core = lax.axis_index("tok") % 2
    got[core] = mine[...]
    got[1 - core] = other[...]
    for n in range(images):
        small[n] = got[1, n, :16].astype(F32) + got[1, n, 16:32].astype(F32)
    styles = jnp.concatenate(
        [small[:, 10], small[:, 11], jnp.zeros((C - 2 * images, C), F32)], axis=0
    )
    flip[...] = styles.T
    shard = lax.axis_index("samp")
    style_c = flip[pl.ds(pl.multiple_of(shard * width, 8), width)]
    for n in range(images):
        last = small[n, 15:16]
        style = style_c[:, n : n + 1][None]
        d_style = style_c[:, images + n : images + n + 1][None]
        row_p, row_d, row_k = (small[n, j : j + 1][None] for j in (12, 13, 14))
        rest = got[1, n, 32:].astype(F32)[: (TAPS - split) * width]
        proj = jnp.concatenate([got[0, n].astype(F32), rest], axis=0).reshape(TAPS, width, C)
        mixed = last[:, 32:33][None] * bank_s[0]
        d_mixed = last[:, 40:41][None] * bank_s[0]
        for b in range(1, NB):
            mixed = mixed + last[:, 32 + b : 33 + b][None] * bank_s[b]
            d_mixed = d_mixed + last[:, 40 + b : 41 + b][None] * bank_s[b]
        scaled = mixed * style
        d_scaled = d_mixed * style + mixed * d_style
        second = row_p * proj + row_d * d_scaled + row_k * scaled
        to_k[n] = second * style + proj * d_style
        to_dk[n] = proj * style
    for b in range(NB):
        total = jnp.zeros((TAPS, width, C), F32)
        for n in range(images):
            last = small[n, 15:16]
            total = total + last[:, 16 + b : 17 + b][None] * to_k[n]
            total = total + last[:, 24 + b : 25 + b][None] * to_dk[n]
        bank_grad[b] = total
    last = small[:, 15]
    right = jnp.concatenate(
        [
            jnp.concatenate([small[:, 8], last], axis=1),
            jnp.concatenate([small[:, 9], pltpu.roll(last, C - NB, 1)], axis=1),
        ],
        axis=0,
    )
    for j in range(4):
        left = jnp.concatenate([small[:, j], small[:, 4 + j]], axis=0)
        both = lax.dot_general(
            left, right, (((0,), (0,)), ((), ())), precision=HIGH, preferred_element_type=F32
        )
        style_grad[C * j : C * j + C] = both[:, :C]
        select_grad[:, C * j : C * j + C] = both[:, C:].T[:NB]


def neighbour_rows(block):
    count = lax.axis_size("tok")
    core = lax.axis_index("tok") % 2
    first, last = block[:1], block[block.shape[0] - 1 :]
    swap = [(i, i ^ 1) for i in range(count)]
    pairs = [(i, i + 1) for i in range(1, count - 1, 2)]
    pairs = pairs + [(b, a) for a, b in pairs]
    far = lax.ppermute(jnp.where(core == 0, first, last), "tok", pairs)
    near = lax.ppermute(jnp.where(core == 0, last, first), "tok", swap)
    return near, far


def local(features_in, path_noise, latent, bank, style_weight, select_weight, path_mean):
    _, rows, cols, chans = features_in.shape
    images = lax.axis_size("samp")
    toks = lax.axis_size("tok")
    width = chans // images
    swap = [(i, i ^ 1) for i in range(toks)]
    scale = 1.0 / math.sqrt(rows * toks * cols)
    block, noise = features_in[0], path_noise[0]
    near, far = neighbour_rows(block)
    cube = (TAPS, C, C)
    select_t = select_weight.T
    taps, small = call(
        kernel_maker,
        [((4 * C, 6 * C), BF16), ((8, C), F32)],
        [latent, bank, style_weight, select_t],
        [pltpu.VMEM(cube, F32)],
        flops=2_000_000_000,
        name="kernel_maker",
    )
    half = TAPS * C // 2
    edge = ((3 * C, cols), BF16)
    flat, edge_low, edge_high = call(
        corr_kernel,
        [((TAPS * C, C), F32), edge, edge],
        [block, noise],
        [
            pltpu.VMEM((3 * C, 3 * C), F32),
            pltpu.VMEM(block.shape, BF16),
            pltpu.VMEM(noise.shape, BF16),
            pltpu.SemaphoreType.DMA((2, rows // GROUP)),
        ],
        flops=4_000_000_000,
        name="corr",
        far=(0, 1),
        limit=CORR_LIMIT,
    )
    keep, give = call(
        edge_kernel,
        [((half, C), F32)] * 2,
        [near, far, flat, edge_low, edge_high],
        [pltpu.VMEM((TAPS * C, C), F32)],
        flops=500_000_000,
        name="edge",
    )
    given = lax.ppermute(give, "tok", swap)
    quarter = ((half // 4, C), F32)

    def along_y(step):
        return [(i, i // 8 * 8 + (i + 2 * step) % 8) for i in range(toks)]

    own, *out = call(split_kernel, [quarter] * 4, [keep, given, small], name="split")
    features, token = conv_part(0, 3, near, far, block, taps, own, None)
    came = [lax.ppermute(out[j - 1], "tok", along_y(j)) for j in (2, 1, 3)]
    (own,) = call(add_kernel, [quarter], [own, *came, token], name="add_y")
    features, token = conv_part(3, 2, near, far, block, taps, own, features)
    came = lax.ppermute(own, "tok", [(i, i ^ 8) for i in range(toks)])
    (own,) = call(add_kernel, [quarter], [own, came, token], name="add_x")
    features, token = conv_part(5, 3, near, far, block, taps, own, features)
    came = [lax.ppermute(own, "tok", along_y(j)) for j in (2, 1, 3)]
    came = [came[1], came[0], came[2]]
    (mine,) = call(
        gather_kernel, [((half, C), F32)], [own, *came, token], name="gather_y"
    )
    other = lax.ppermute(mine, "tok", swap)
    shard = lax.axis_index("samp")
    bank_s = lax.dynamic_slice_in_dim(bank, shard * width, width, 2).astype(F32)
    message = (TAPS - 1) * width

    def image(*refs):
        image_kernel(scale, images, *refs)

    sent, penalty = call(
        image,
        [((images, message, C), BF16), ((1, 1), F32)],
        [
            mine, other, small, latent, bank, style_weight, select_t,
            path_mean.reshape(1, 1), bank_s,
        ],
        [
            pltpu.VMEM(cube, F32),
            pltpu.VMEM(cube, F32),
            pltpu.VMEM((TAPS * C, C), F32),
            pltpu.VMEM(cube, F32),
            pltpu.VMEM(cube, F32),
            pltpu.VMEM(cube, F32),
            pltpu.VMEM(cube, F32),
        ],
        flops=6_000_000_000,
        name="image",
        limit=16,
    )
    got = lax.all_to_all(sent, "samp", 0, 0)
    got_other = lax.ppermute(got, "tok", swap)
    bank_grad, style_grad, select_grad = call(
        final_kernel,
        [((NB, TAPS, width, C), F32), (style_weight.shape, F32), (select_weight.shape[::-1], F32)],
        [got, got_other, bank_s],
        [
            pltpu.VMEM((2, images, message, C), BF16),
            pltpu.VMEM((images, 16, C), F32),
            pltpu.VMEM((C, C), F32),
            pltpu.VMEM((images, TAPS, width, C), F32),
            pltpu.VMEM((images, TAPS, width, C), F32),
        ],
        name="final",
    )
    return (features[None], penalty.reshape(1), bank_grad, style_grad, select_grad.T)


def solution(mesh):
    placed = (
        P("samp", "tok", None, None),
        P("samp", "tok", None, None),
        P("samp", None),
        P(),
        P(),
        P(),
        P(),
    )
    return jax.shard_map(
        local,
        mesh=mesh,
        in_specs=placed,
        out_specs=(P("samp", "tok", None, None), P("samp"), P(None, None, "samp", None), P(), P()),
        check_vma=False,
    )
```
